128 devices in a mesh: grp: 4 (over y_hi, core), blk: 32 (over z, x, y_lo).
Axes of the slice: x: 4, y: 4 (y_hi: 2, y_lo: 2; y = y_hi * 2 + y_lo), z: 4, core: 2. Of those that a mesh axis runs over, the one named last changes fastest.
Arguments:
- embeds: bfloat16 [4, 32768, 1024], P('grp', 'blk')
- doc_ids: int32 [4, 32768], P('grp', 'blk'), may hold values from 0 to 32767, each once within a row
- prior_max: float32 [4, 32768], P('grp', 'blk'), may hold values from -0.2 to 0.6
- owned: bfloat16 [32768, 1024], P(('grp', 'blk')), may hold values from -6 to 6
- owned_ids: int32 [32768], P(('grp', 'blk')), may hold values from 0 to 32767, each once
- owner_dest: int32 [32768, 1], P(('grp', 'blk')), may hold values from 0 to 127; in each aligned block of 256 rows (0 to 255, 256 to 511, ...) at most 4 rows name the same one
Outputs:
- running_max: float32 [4, 32768], P('grp', 'blk')
- next_rows: bfloat16 [65536, 1024], P(('grp', 'blk'))
- next_ids: int32 [65536], P(('grp', 'blk'))
The draws below stay inside these ranges and needn't reach their ends.
Inputs may be any that keep to these rules, and one draw needn't show every extreme that they name: `owner_dest`: among the 256 rows of one device no target is named more than 4 times, a bound that some block reaches.
All inputs are finite; a program needn't handle non-finite values.
Results may differ from the reference program's by a relative error of at most 0.0016.
Values may be sent and summed in bfloat16 or wider, within the bound.
No kernel may reach another device: no remote copies, remote signals or barrier semaphores. Data moves between devices by JAX's collectives and lax.ppermute only.
A program may use at most 64 MiB of HBM per device.

```python
import math
import jax
import jax.numpy as jnp
import numpy as np
from jax import lax

E = 1024
ROWS_DEV = 1024
CYCLE = 3
CAP = 4
CR = 32768
OWN_DEV = 256
TOTAL_OWN = 32768
SLOTS = 512
N_GRP = 4
N_BLK = 32
DEVICES = 128


def draw_embeds(key, part):
    keys = jax.random.split(jax.random.fold_in(key, 7), 4)
    nblk = CR // ROWS_DEV
    base = jax.random.normal(keys[0], (N_GRP, CR, E), jnp.float32)
    offset = jax.random.randint(keys[1], (N_GRP, CR), 0, CYCLE + 1)
    within = jax.random.randint(keys[2], (N_GRP, CR), 0, ROWS_DEV)
    blocks = jnp.arange(CR, dtype=jnp.int32)[None, :] // ROWS_DEV
    partner = (blocks - offset) % nblk * ROWS_DEV + within
    partner_rows = jnp.take_along_axis(base, partner[:, :, None], axis=1)
    weight = jnp.exp(jax.random.uniform(keys[3], (N_GRP, CR, 1), jnp.float32, jnp.log(0.3), jnp.log(3.0)))
    result = base + weight * partner_rows
    return result.astype(jnp.bfloat16)


def levels(own_key, shape, pieces, smallest, high):
    def one(dim, blocks):
        draws = jax.random.uniform(jax.random.fold_in(jax.random.fold_in(own_key, 6), dim), (blocks,), jnp.float32, smallest / len(pieces), high / len(pieces))
        return jnp.repeat(jnp.exp(draws), shape[dim] // blocks).reshape((-1,) + (1,) * (len(shape) - dim - 1))

    gain = one(*pieces[0])
    for cut in pieces[1:]:
        gain = gain * one(*cut)
    return gain


def deal_out(key, own, number, rows, number_of, top, limit, lean):
    order = jax.random.permutation(key, number_of)
    heavy_load, ordinary = load_shares(number_of, rows * top, limit, lean, True), load_shares(number_of, rows * top, limit, lean, False)
    places = jnp.arange(number_of)

    def named(sizes, turn):
        used = int((sizes > 0).sum())
        fixed = max(1, used // 4)
        moved = fixed + (places - fixed + turn * (used - fixed)) % max(1, number_of - fixed)
        return jnp.zeros((number_of,), jnp.int32).at[order[jnp.where(places < fixed, places, moved)]].set(jnp.asarray(sizes, jnp.int32))

    sizes = jnp.where(number % 4 == 0, named(heavy_load, number // 4), named(ordinary, number - number // 4 - 1))
    mixed = jax.random.permutation(jax.random.fold_in(own, 3), number_of)
    giver, taker = mixed[0:number_of // 2 * 2:2], mixed[1:number_of // 2 * 2:2]
    room = jnp.minimum(sizes[giver] - 1, limit - sizes[taker]) // 2
    room = jnp.where((giver == order[0]) | (taker == order[0]) | (sizes[taker] == 0), 0, jnp.maximum(room, 0))
    moved = jax.random.randint(jax.random.fold_in(own, 4), (number_of // 2,), 0, 1 << 20) % (room + 1)
    sizes = sizes.at[giver].add(-moved).at[taker].add(moved)
    items = jnp.searchsorted(jnp.cumsum(sizes), jnp.arange(rows * top), side="right").astype(jnp.int32)
    grid = items.reshape(top, rows).T
    grid = grid[jax.random.permutation(jax.random.fold_in(own, 1), rows)]
    turn = jax.random.randint(jax.random.fold_in(own, 2), (rows, 1), 0, top)
    return jnp.take_along_axis(grid, (jnp.arange(top)[None, :] + turn) % top, axis=1)


def load_shares(number_of, total, reach, skew, full):
    loads = [(1 << 20) // math.isqrt(standing ** skew) + 1 for standing in range(1, number_of + 1)]
    largest = reach if full else min(reach, max(-(-total // number_of), total * loads[0] // sum(loads)))
    least = 1 if total - largest >= number_of - 1 else 0
    given, surplus = [largest] + [least] * (number_of - 1), total - largest - least * (number_of - 1)
    while surplus > 0:
        free = [i for i in range(1, number_of) if given[i] < largest] or [i for i in range(1, number_of) if given[i] < reach]
        mass, left = sum([loads[i] for i in free]), surplus
        for i in free:
            addition = min(reach - given[i], max(1, left * loads[i] // mass), surplus)
            given[i] = given[i] + addition
            surplus = surplus - addition
    return np.array(given)


def noise(key, extent, spread, bound, cuts=(), held_as=jnp.bfloat16):
    gain = levels(key, extent, cuts, -0.22, 0.18) if cuts else 1.0
    array = jax.random.normal(key, extent, jnp.float32) * spread * gain
    return jnp.minimum(jnp.maximum(array, -bound), bound).astype(held_as)


def setup_inputs(seed: int = 0) -> dict:
    key_list = jax.random.split(jax.random.key(seed), 7)
    embeds = draw_embeds(jax.random.fold_in(key_list[6], 71), 0)
    doc_ids = jax.vmap(lambda own: jax.random.permutation(own, CR))(jax.random.split(key_list[1], N_GRP)).reshape((N_GRP, CR)).astype(jnp.int32)
    prior_max = jnp.clip(-0.2 + 0.8 * jax.random.uniform(key_list[2], (N_GRP, CR), jnp.float32) ** levels(key_list[2], (N_GRP, CR), ((0, 4), (1, 32)), -0.2, 0.2), -0.2, 0.6)
    owned = noise(key_list[3], (TOTAL_OWN, E), 1.0, 6.0, ((0, 128),))
    owned_ids = jax.random.permutation(key_list[4], TOTAL_OWN).astype(jnp.int32)
    owner_dest_keys = jax.random.split(jax.random.fold_in(key_list[5], 1), TOTAL_OWN // OWN_DEV)
    owner_dest_turns = jax.random.permutation(jax.random.fold_in(key_list[5], 3), TOTAL_OWN // OWN_DEV)
    owner_dest = jax.vmap(lambda own, number: deal_out(jax.random.fold_in(key_list[5], 2), own, number, OWN_DEV, DEVICES, 1, CAP, 2))(owner_dest_keys, owner_dest_turns).reshape((TOTAL_OWN, 1))
    return {"embeds": embeds, "doc_ids": doc_ids, "prior_max": prior_max, "owned": owned, "owned_ids": owned_ids, "owner_dest": owner_dest}


def normalize(matrix):
    values = matrix.astype(jnp.float32)
    scale = lax.rsqrt(lax.optimization_barrier(jnp.sum(values * values, axis=-1, keepdims=True)) + 1e-06)
    return (values * scale).astype(jnp.bfloat16)

def tile_max(operands):
    row_normed, row_ids, col_normed, col_ids = operands
    scores = lax.dot_general(row_normed, col_normed, (((1,), (1,)), ((), ())), preferred_element_type=jnp.float32)
    masked = jnp.where(col_ids[None, :] < row_ids[:, None], scores, jnp.float32(-2.0))
    return lax.optimization_barrier(jnp.max(masked, axis=1))

def reference(embeds, doc_ids, prior_max, owned, owned_ids, owner_dest):
    normed = normalize(embeds).reshape(N_GRP, N_BLK, ROWS_DEV, E)
    numbers = doc_ids.reshape(N_GRP, N_BLK, ROWS_DEV)
    running = prior_max.reshape(N_GRP, N_BLK, ROWS_DEV).astype(jnp.float32)
    for distance in range(CYCLE + 1):
        col_normed = jnp.roll(normed, distance, axis=1)
        col_ids = jnp.roll(numbers, distance, axis=1)
        found = lax.map(tile_max, (normed.reshape(-1, ROWS_DEV, E), numbers.reshape(-1, ROWS_DEV), col_normed.reshape(-1, ROWS_DEV, E), col_ids.reshape(-1, ROWS_DEV)))
        running = jnp.maximum(running, found.reshape(N_GRP, N_BLK, ROWS_DEV))
    running_max = running.reshape(N_GRP, CR)
    devices = N_GRP * N_BLK
    owned_normed = normalize(owned)
    target = owner_dest[:, 0].astype(jnp.int32)
    grouped = target.reshape(devices, OWN_DEV)
    onehot = (grouped[:, :, None] == jnp.arange(devices, dtype=jnp.int32)[None, None, :]).astype(jnp.int32)
    position = lax.optimization_barrier(jnp.sum(jnp.cumsum(onehot, axis=1) * onehot, axis=2)) - 1
    source = jnp.arange(devices, dtype=jnp.int32)[:, None]
    place = (grouped * SLOTS + source * CAP + position).reshape(-1).astype(jnp.int32)
    next_rows = jnp.zeros((devices * SLOTS, E), jnp.bfloat16).at[place].set(owned_normed)
    next_ids = jnp.full((devices * SLOTS,), -1, jnp.int32).at[place].set(owned_ids.astype(jnp.int32))
    return (running_max, next_rows, next_ids)
```

```python
import jax
import jax.numpy as jnp
from jax import lax
from jax.experimental import pallas as pl
from jax.experimental.pallas import tpu as pltpu
from jax.sharding import PartitionSpec as P

CAP = 4
PARTS = 4
LOWEST = -2.0
BOTH = ("grp", "blk")


def normalize(matrix):
    values = matrix.astype(jnp.float32)
    scale = lax.rsqrt(jnp.sum(values * values, axis=-1, keepdims=True) + 1e-06)
    return (values * scale).astype(jnp.bfloat16)


def send(value, to):
    count = lax.axis_size("blk")
    pairs = [(s, to(s) % count) for s in range(count) if to(s) is not None]
    return lax.ppermute(value, "blk", pairs)


def params():
    return pltpu.CompilerParams(vmem_limit_bytes=48 * 1024 * 1024)


def vmem(n):
    return [pl.BlockSpec(memory_space=pltpu.VMEM)] * n


def down(row):
    return jnp.broadcast_to(row, (128, row.shape[1])).T


def best(rows, row_ids, cols, col_down):
    scores = lax.dot_general(cols, rows, (((1,), (1,)), ((), ())), preferred_element_type=jnp.float32)
    found = []
    for left in range(0, rows.shape[0], 128):
        keep = col_down < row_ids[:, left : left + 128]
        part = jnp.where(keep, scores[:, left : left + 128], jnp.float32(LOWEST))
        found.append(jnp.max(part, axis=0, keepdims=True))
    return jnp.concatenate(found, axis=1)


def norm_kernel(x_ref, out_ref):
    out_ref[...] = normalize(x_ref[...])


def norm_part(embeds, part):
    rows, width = embeds.shape
    size = rows // PARTS
    return pl.pallas_call(
        norm_kernel,
        grid=(1,),
        in_specs=[pl.BlockSpec((size, width), lambda i: (part, 0))],
        out_specs=pl.BlockSpec((size, width), lambda i: (0, 0)),
        out_shape=jax.ShapeDtypeStruct((size, width), jnp.bfloat16),
        compiler_params=params(),
        name=f"norm_{part}",
        cost_estimate=pl.CostEstimate(flops=4 * size * width, bytes_accessed=4 * size * width, transcendentals=size),
    )(embeds)


def place_kernel(rows_ref, target_ref, out_ref):
    count = rows_ref.shape[0]
    target = target_ref[...]
    across = jnp.broadcast_to(target, (count, count))
    earlier = lax.broadcasted_iota(jnp.int32, (count, count), 0) < lax.broadcasted_iota(
        jnp.int32, (count, count), 1
    )
    same = (across.T == across) & earlier
    position = jnp.sum(same.astype(jnp.float32), axis=0, keepdims=True).astype(jnp.int32)
    place = target * CAP + position
    slots = out_ref.shape[0] * out_ref.shape[1]
    pick = (lax.broadcasted_iota(jnp.int32, (slots, count), 0) == place).astype(jnp.float32).astype(jnp.bfloat16)
    placed = jnp.dot(pick, normalize(rows_ref[...]), preferred_element_type=jnp.float32)
    out_ref[...] = placed.astype(jnp.bfloat16).reshape(out_ref.shape)


def placed_rows(owned, target, devices):
    count, width = owned.shape
    return pl.pallas_call(
        place_kernel,
        in_specs=vmem(2),
        out_specs=pl.BlockSpec(memory_space=pltpu.VMEM),
        out_shape=jax.ShapeDtypeStruct((devices, CAP, width), jnp.bfloat16),
        compiler_params=params(),
        name="place",
        cost_estimate=pl.CostEstimate(
            flops=2 * devices * CAP * count * width, bytes_accessed=2 * (count + devices * CAP) * width, transcendentals=count
        ),
    )(owned, target)


def ids_kernel(numbers, me_ref, all_ref, out_ref):
    me = me_ref[0]
    count = numbers // 2
    ids = all_ref[:, :count].astype(jnp.float32)
    mine = all_ref[:, count:] == me
    ones = mine.astype(jnp.float32)
    earlier = (
        lax.broadcasted_iota(jnp.int32, (count, count), 0) < lax.broadcasted_iota(jnp.int32, (count, count), 1)
    ).astype(jnp.float32)
    position = jnp.dot(
        ones.astype(jnp.bfloat16), earlier.astype(jnp.bfloat16), preferred_element_type=jnp.float32
    )
    found = [
        jnp.sum(jnp.where(mine & (position == p), ids + 1.0, 0.0), axis=1, keepdims=True) - 1.0
        for p in range(CAP)
    ]
    out_ref[...] = jnp.concatenate(found, axis=1).astype(jnp.int32)


def self_kernel(*refs):
    parts, (ids_ref, prior_ref, out_ref, down_ref) = refs[:PARTS], refs[PARTS:]
    size = parts[0].shape[0]
    down_ref[...] = down(ids_ref[...])
    for r in range(PARTS):
        at = slice(r * size, (r + 1) * size)
        found = prior_ref[:, at]
        for c in range(PARTS):
            cols = down_ref[c * size : (c + 1) * size, :]
            found = jnp.maximum(found, best(parts[r][...], ids_ref[:, at], parts[c][...], cols))
        out_ref[:, at] = found


def main_kernel(*refs):
    own, other = refs[:PARTS], refs[PARTS : 2 * PARTS]
    (where_ref, before_ref, ids_ref, other_ids_ref, before_ids_ref, so_far_ref) = refs[2 * PARTS : 2 * PARTS + 6]
    own_out, other_out, before_out, down_ref = refs[2 * PARTS + 6 :]
    size = own[0].shape[0]
    before_out[...] = normalize(before_ref[...])
    down_ref[...] = down(before_ids_ref[...])
    for r in range(PARTS):
        at = slice(r * size, (r + 1) * size)
        found = best(own[r][...], ids_ref[:, at], before_out[...], down_ref[...])
        own_out[:, at] = jnp.maximum(so_far_ref[:, at], found)
    for r in range(PARTS):
        at = slice(r * size, (r + 1) * size)
        other_out[:, at] = best(other[r][...], other_ids_ref[:, at], before_out[...], down_ref[...])

    @pl.when(where_ref[0] == 0)
    def _():
        down_ref[...] = down(ids_ref[...])
        for r in range(PARTS):
            at = slice(r * size, (r + 1) * size)
            found = other_out[:, at]
            for c in range(PARTS):
                cols = down_ref[c * size : (c + 1) * size, :]
                found = jnp.maximum(found, best(other[r][...], other_ids_ref[:, at], own[c][...], cols))
            other_out[:, at] = found


def far_kernel(parts, *refs):
    rows, (where_ref, before_ref, row_ids_ref, before_ids_ref, out_ref, down_ref) = refs[:parts], refs[parts:]
    size = rows[0].shape[0]

    @pl.when(where_ref[0] == 1)
    def _():
        down_ref[...] = down(before_ids_ref[...])
        for r in range(parts):
            at = slice(r * size, (r + 1) * size)
            out_ref[:, at] = best(rows[r][...], row_ids_ref[:, at], before_ref[...], down_ref[...])

    @pl.when(where_ref[0] == 0)
    def _():
        out_ref[...] = jnp.full(out_ref.shape, LOWEST, jnp.float32)


def far(rows, where, before, row_ids, before_ids):
    parts = len(rows)
    size, width = rows[0].shape
    cols = before.shape[0]
    return pl.pallas_call(
        lambda *refs: far_kernel(parts, *refs),
        in_specs=vmem(parts) + [pl.BlockSpec(memory_space=pltpu.SMEM)] + vmem(3),
        out_specs=pl.BlockSpec(memory_space=pltpu.VMEM),
        out_shape=jax.ShapeDtypeStruct((1, parts * size), jnp.float32),
        scratch_shapes=[pltpu.VMEM((cols, 128), jnp.int32)],
        compiler_params=params(),
        name=f"far_{parts}",
        cost_estimate=pl.CostEstimate(
            flops=2 * parts * size * cols * width, bytes_accessed=2 * (parts * size + cols) * width, transcendentals=0
        ),
    )(*rows, where, before, row_ids, before_ids)


def body(embeds, doc_ids, prior_max, owned, owned_ids, owner_dest):
    members = lax.axis_size("blk")
    devices = lax.axis_size("grp") * members
    raw = embeds[0]
    rows, width = raw.shape
    size = rows // PARTS
    group, member = lax.axis_index("grp"), lax.axis_index("blk")
    where = (member % 2).astype(jnp.int32).reshape(1)

    before = send(raw, lambda s: s + 2)
    numbers = jnp.concatenate([doc_ids[0], owned_ids, owner_dest[:, 0]])
    everyone = lax.all_gather(numbers, BOTH)

    own, other, after = [], [], []
    for part in range(PARTS):
        own.append(norm_part(raw, part))
        other.append(send(own[part], lambda s: s ^ 1))
        after.append(send(other[part], lambda s: s - 2 if s % 2 else None))

    outgoing = placed_rows(owned, owner_dest.reshape(1, -1), devices)
    arrived = lax.all_to_all(outgoing, BOTH, split_axis=0, concat_axis=0, tiled=True)
    next_rows = arrived.reshape(devices * CAP, width)

    me = (group * members + member).astype(jnp.int32)
    owners = everyone[:, rows:]
    next_ids = pl.pallas_call(
        lambda *refs: ids_kernel(owners.shape[1], *refs),
        in_specs=[pl.BlockSpec(memory_space=pltpu.SMEM)] + vmem(1),
        out_specs=pl.BlockSpec(memory_space=pltpu.VMEM),
        out_shape=jax.ShapeDtypeStruct((devices, CAP), jnp.int32),
        compiler_params=params(),
        name="ids",
    )(me.reshape(1), owners).reshape(devices * CAP)

    def ids_of(number):
        return lax.dynamic_slice(everyone, (group * members + number % members, 0), (1, rows))

    other_ids = ids_of(member + 1 - 2 * (member % 2))
    before_ids = ids_of(member + members - 2)
    after_ids = ids_of(member + 1)

    mine = pl.pallas_call(
        self_kernel,
        in_specs=vmem(PARTS + 2),
        out_specs=pl.BlockSpec(memory_space=pltpu.VMEM),
        out_shape=jax.ShapeDtypeStruct((1, rows), jnp.float32),
        scratch_shapes=[pltpu.VMEM((rows, 128), jnp.int32)],
        compiler_params=params(),
        name="within",
        cost_estimate=pl.CostEstimate(flops=2 * rows * rows * width, bytes_accessed=2 * rows * width, transcendentals=0),
    )(*own, doc_ids, prior_max)

    mine, others, before_normed = pl.pallas_call(
        main_kernel,
        in_specs=vmem(2 * PARTS) + [pl.BlockSpec(memory_space=pltpu.SMEM)] + vmem(5),
        out_specs=vmem(3),
        out_shape=[
            jax.ShapeDtypeStruct((1, rows), jnp.float32),
            jax.ShapeDtypeStruct((1, rows), jnp.float32),
            jax.ShapeDtypeStruct((rows, width), jnp.bfloat16),
        ],
        scratch_shapes=[pltpu.VMEM((rows, 128), jnp.int32)],
        compiler_params=params(),
        name="across",
        cost_estimate=pl.CostEstimate(
            flops=6 * rows * rows * width, bytes_accessed=8 * rows * width, transcendentals=rows
        ),
    )(*own, *other, where, before, doc_ids, other_ids, before_ids, mine)
    from_other = send(others, lambda s: s ^ 1)

    early = far(after[: PARTS - 1], where, before_normed, after_ids[:, : rows - size], before_ids)
    late = far(after[PARTS - 1 :], where, before_normed, after_ids[:, rows - size :], before_ids)
    from_far = send(jnp.concatenate([early, late], axis=1), lambda s: s + 1 if s % 2 else None)
    from_far = jnp.where(where[0] == 0, from_far, jnp.float32(LOWEST))
    running = jnp.maximum(jnp.maximum(mine, from_other), from_far)
    return (running, next_rows, next_ids)


def solution(mesh):
    return jax.shard_map(
        body,
        mesh=mesh,
        in_specs=(
            P("grp", "blk", None),
            P("grp", "blk"),
            P("grp", "blk"),
            P(("grp", "blk"), None),
            P(("grp", "blk")),
            P(("grp", "blk"), None),
        ),
        out_specs=(P("grp", "blk"), P(("grp", "blk"), None), P(("grp", "blk"))),
        check_vma=False,
    )
```

```python
import jax
import jax.numpy as jnp
from jax import lax
from jax.experimental import pallas as pl
from jax.experimental.pallas import tpu as pltpu
from jax.sharding import PartitionSpec as P

CAP = 4
PARTS = 4
LOWEST = -2.0
EXTRA = 16
BOTH = ("grp", "blk")


def normalize(matrix):
    values = matrix.astype(jnp.float32)
    scale = lax.rsqrt(jnp.sum(values * values, axis=-1, keepdims=True) + 1e-06)
    return (values * scale).astype(jnp.bfloat16)


def send(value, to):
    count = lax.axis_size("blk")
    pairs = [(s, to(s) % count) for s in range(count) if to(s) is not None]
    return lax.ppermute(value, "blk", pairs)


def params():
    return pltpu.CompilerParams(vmem_limit_bytes=48 * 1024 * 1024)


def vmem(n):
    return [pl.BlockSpec(memory_space=pltpu.VMEM)] * n


def down(row):
    return jnp.broadcast_to(row, (128, row.shape[1])).T


def best(rows, row_ids, cols, col_down):
    scores = lax.dot_general(cols, rows, (((1,), (1,)), ((), ())), preferred_element_type=jnp.float32)
    found = []
    for left in range(0, rows.shape[0], 128):
        keep = col_down < row_ids[:, left : left + 128]
        part = jnp.where(keep, scores[:, left : left + 128], jnp.float32(LOWEST))
        found.append(jnp.max(part, axis=0, keepdims=True))
    return jnp.concatenate(found, axis=1)


def halves(numbers):
    numbers = numbers.astype(jnp.int32)
    return (numbers >> 7).astype(jnp.float32), (numbers & 127).astype(jnp.float32)


def number_rows(ref):
    tail = ref[ref.shape[0] - EXTRA :, :].astype(jnp.float32)
    return (tail[0:1, :] * 128.0 + tail[1:2, :]).astype(jnp.int32)


def tail_rows(ids, width):
    ids = jnp.concatenate([ids, jnp.zeros((1, width - ids.shape[1]), jnp.int32)], axis=1) if ids.shape[1] < width else ids
    high, low = halves(ids)
    row = lax.broadcasted_iota(jnp.int32, (EXTRA, width), 0)
    return jnp.where(row == 0, high, jnp.where(row == 1, low, 0.0)).astype(jnp.bfloat16)


def first_kernel(x_ref, ids_ref, out_ref):
    size, width = x_ref.shape
    out_ref[:size, :] = normalize(x_ref[...])
    out_ref[size:, :] = tail_rows(ids_ref[:, :size], width)


def rest_kernel(x_ref, ids_ref, first_ref, *outs):
    whole_ref = outs[-1]
    rows, width = x_ref.shape
    size = rows // PARTS
    whole_ref[:size, :] = first_ref[:size, :]
    for part in range(1, PARTS):
        at = slice(part * size, (part + 1) * size)
        normed = normalize(x_ref[at, :])
        outs[part - 1][:size, :] = normed
        outs[part - 1][size:, :] = tail_rows(ids_ref[:, at], width)
        whole_ref[at, :] = normed
    whole_ref[rows:, :] = tail_rows(ids_ref[...], width)


def norm_parts(embeds, ids):
    rows, width = embeds.shape
    size = rows // PARTS

    def cost(part):
        return pl.CostEstimate(flops=4 * part * width, bytes_accessed=4 * part * width, transcendentals=part)

    def shape(part):
        return jax.ShapeDtypeStruct((part, width), jnp.bfloat16)

    first = pl.pallas_call(
        first_kernel,
        grid=(1,),
        in_specs=[
            pl.BlockSpec((size, width), lambda i: (0, 0)),
            pl.BlockSpec((1, rows), lambda i: (0, 0)),
        ],
        out_specs=pl.BlockSpec((size + EXTRA, width), lambda i: (0, 0)),
        out_shape=shape(size + EXTRA),
        compiler_params=params(),
        name="norm_first",
        cost_estimate=cost(size),
    )(embeds, ids)
    rest = pl.pallas_call(
        rest_kernel,
        in_specs=vmem(3),
        out_specs=vmem(PARTS),
        out_shape=[shape(size + EXTRA)] * (PARTS - 1) + [shape(rows + EXTRA)],
        compiler_params=params(),
        name="norm_rest",
        cost_estimate=cost(rows),
    )(embeds, ids, first)
    return [first, *rest[:-1]], rest[-1]


def place_kernel(rows_ref, target_ref, ids_ref, out_ref):
    count, width = rows_ref.shape
    target = target_ref[...]
    across = jnp.broadcast_to(target, (count, count))
    earlier = lax.broadcasted_iota(jnp.int32, (count, count), 0) < lax.broadcasted_iota(
        jnp.int32, (count, count), 1
    )
    same = (across.T == across) & earlier
    position = jnp.sum(same.astype(jnp.float32), axis=0, keepdims=True).astype(jnp.int32)
    place = target * CAP + position
    devices = out_ref.shape[0]
    slots = devices * CAP
    pick = (lax.broadcasted_iota(jnp.int32, (slots, count), 0) == place).astype(jnp.float32).astype(jnp.bfloat16)
    placed = jnp.dot(pick, normalize(rows_ref[...]), preferred_element_type=jnp.float32)
    out_ref[:, :, :width] = placed.astype(jnp.bfloat16).reshape(devices, CAP, width)
    high, low = halves(down(ids_ref[...]))
    lane = lax.broadcasted_iota(jnp.int32, high.shape, 1)
    pair = jnp.where(lane < 64, high + 1.0, low).astype(jnp.bfloat16)
    tail = jnp.dot(pick, pair, preferred_element_type=jnp.float32)
    out_ref[:, :, width:] = tail.astype(jnp.bfloat16).reshape(devices, CAP, 128)


def placed_rows(owned, target, ids, devices):
    count, width = owned.shape
    return pl.pallas_call(
        place_kernel,
        in_specs=vmem(3),
        out_specs=pl.BlockSpec(memory_space=pltpu.VMEM),
        out_shape=jax.ShapeDtypeStruct((devices, CAP, width + 128), jnp.bfloat16),
        compiler_params=params(),
        name="place",
        cost_estimate=pl.CostEstimate(
            flops=2 * devices * CAP * count * width, bytes_accessed=2 * (count + devices * CAP) * width, transcendentals=count
        ),
    )(owned, target, ids)


def split_kernel(in_ref, rows_ref, ids_ref):
    slots, width = rows_ref.shape
    rows_ref[...] = in_ref[:, :, :width].reshape(slots, width)
    tail = in_ref[:, :, width:].reshape(slots, 128).astype(jnp.float32).T
    high, low = tail[0:1, :], tail[64:65, :]
    ids_ref[...] = jnp.where(high == 0.0, -1.0, (high - 1.0) * 128.0 + low).astype(jnp.int32)


def split_rows(arrived):
    devices, cap, wide = arrived.shape
    slots, width = devices * cap, wide - 128
    return pl.pallas_call(
        split_kernel,
        in_specs=vmem(1),
        out_specs=vmem(2),
        out_shape=[
            jax.ShapeDtypeStruct((slots, width), jnp.bfloat16),
            jax.ShapeDtypeStruct((1, slots), jnp.int32),
        ],
        compiler_params=params(),
        name="split",
        cost_estimate=pl.CostEstimate(flops=0, bytes_accessed=4 * slots * width, transcendentals=0),
    )(arrived)


def self_kernel(whole_ref, ids_ref, prior_ref, out_ref, down_ref):
    rows = ids_ref.shape[1]
    size = rows // PARTS
    down_ref[...] = down(ids_ref[...])
    out_ref[...] = prior_ref[...]
    parts = [whole_ref.at[r * size : (r + 1) * size, :] for r in range(PARTS)]
    against(parts, ids_ref[...], whole_ref[:rows, :], down_ref, out_ref)


def against(row_refs, row_ids, cols, down_ref, out_ref):
    size = out_ref.shape[1] // len(row_refs)
    for r, rows in enumerate(row_refs):
        at = slice(r * size, (r + 1) * size)
        found = best(rows[:size, :], row_ids[:, at], cols, down_ref[...])
        out_ref[:, at] = jnp.maximum(out_ref[:, at], found)


def main_kernel(*refs):
    own, other = refs[:PARTS], refs[PARTS : 2 * PARTS]
    whole_ref, before_ref, where_ref, ids_ref, so_far_ref, own_out, other_out, down_ref = refs[2 * PARTS :]
    rows = ids_ref.shape[1]
    size = rows // PARTS
    other_ids = jnp.concatenate([number_rows(part)[:, :size] for part in other], axis=1)
    down_ref[...] = down(number_rows(before_ref))
    own_out[...] = so_far_ref[...]
    other_out[...] = jnp.full(other_out.shape, LOWEST, jnp.float32)
    against(own, ids_ref[...], before_ref[:rows, :], down_ref, own_out)
    against(other, other_ids, before_ref[:rows, :], down_ref, other_out)

    @pl.when(where_ref[0] == 0)
    def _():
        down_ref[...] = down(ids_ref[...])
        against(other, other_ids, whole_ref[:rows, :], down_ref, other_out)


def far_kernel(part, rows_ref, before_ref, where_ref, so_far_ref, out_ref, down_ref):
    rows = out_ref.shape[1]
    size = rows // PARTS
    out_ref[...] = so_far_ref[...]

    @pl.when(where_ref[0] == 1)
    def _():
        down_ref[...] = down(number_rows(before_ref))
        at = slice(part * size, (part + 1) * size)
        against([rows_ref], number_rows(rows_ref)[:, :size], before_ref[:rows, :], down_ref, out_ref.at[:, at])


def far(after, where, before):
    size, width = after[0].shape
    rows = PARTS * (size - EXTRA)
    found = jnp.full((1, rows), LOWEST, jnp.float32)
    for part in range(PARTS):
        found = pl.pallas_call(
            lambda *refs, part=part: far_kernel(part, *refs),
            in_specs=vmem(2) + [pl.BlockSpec(memory_space=pltpu.SMEM)] + vmem(1),
            out_specs=pl.BlockSpec(memory_space=pltpu.VMEM),
            out_shape=jax.ShapeDtypeStruct((1, rows), jnp.float32),
            scratch_shapes=[pltpu.VMEM((rows, 128), jnp.int32)],
            compiler_params=params(),
            name=f"far_{part}",
            cost_estimate=pl.CostEstimate(
                flops=2 * size * rows * width, bytes_accessed=2 * (size + rows) * width, transcendentals=0
            ),
        )(after[part], before, where, found)
    return found


def body(embeds, doc_ids, prior_max, owned, owned_ids, owner_dest):
    members = lax.axis_size("blk")
    devices = lax.axis_size("grp") * members
    raw = embeds[0]
    rows, width = raw.shape
    where = (lax.axis_index("blk") & 1).astype(jnp.int32).reshape(1)

    own, whole = norm_parts(raw, doc_ids)
    other = [send(part, lambda s: s ^ 1) for part in own]
    before = send(whole, lambda s: s + 2)
    after = [send(part, lambda s: s - 2 if s % 2 else None) for part in other]

    outgoing = placed_rows(owned, owner_dest.reshape(1, -1), owned_ids.reshape(1, -1), devices)
    next_rows, next_ids = split_rows(lax.all_to_all(outgoing, BOTH, split_axis=0, concat_axis=0, tiled=True))

    mine = pl.pallas_call(
        self_kernel,
        in_specs=vmem(3),
        out_specs=pl.BlockSpec(memory_space=pltpu.VMEM),
        out_shape=jax.ShapeDtypeStruct((1, rows), jnp.float32),
        scratch_shapes=[pltpu.VMEM((rows, 128), jnp.int32)],
        compiler_params=params(),
        name="within",
        cost_estimate=pl.CostEstimate(flops=2 * rows * rows * width, bytes_accessed=2 * rows * width, transcendentals=0),
    )(whole, doc_ids, prior_max)

    mine, others = pl.pallas_call(
        main_kernel,
        in_specs=vmem(2 * PARTS + 2) + [pl.BlockSpec(memory_space=pltpu.SMEM)] + vmem(2),
        out_specs=vmem(2),
        out_shape=[jax.ShapeDtypeStruct((1, rows), jnp.float32)] * 2,
        scratch_shapes=[pltpu.VMEM((rows, 128), jnp.int32)],
        compiler_params=params(),
        name="across",
        cost_estimate=pl.CostEstimate(flops=6 * rows * rows * width, bytes_accessed=6 * rows * width, transcendentals=0),
    )(*own, *other, whole, before, where, doc_ids, mine)
    from_other = send(others, lambda s: s ^ 1)

    from_far = send(far(after, where, before), lambda s: s + 1 if s % 2 else None)
    from_far = jnp.where(where[0] == 0, from_far, jnp.float32(LOWEST))
    running = jnp.maximum(jnp.maximum(mine, from_other), from_far)
    return (running, next_rows, next_ids.reshape(-1))


def solution(mesh):
    return jax.shard_map(
        body,
        mesh=mesh,
        in_specs=(
            P("grp", "blk", None),
            P("grp", "blk"),
            P("grp", "blk"),
            P(("grp", "blk"), None),
            P(("grp", "blk")),
            P(("grp", "blk"), None),
        ),
        out_specs=(P("grp", "blk"), P(("grp", "blk"), None), P(("grp", "blk"))),
        check_vma=False,
    )
```

```python
import jax
import jax.numpy as jnp
from jax import lax
from jax.experimental import pallas as pl
from jax.experimental.pallas import tpu as pltpu
from jax.sharding import PartitionSpec as P

CAP = 4
LOWEST = -2.0
EXTRA = 16
BOTH = ("grp", "blk")
OWN, PARTNER, NEAR, NEAR_PARTNER, FAR_PARTNER = range(5)


def normalize(matrix):
    values = matrix.astype(jnp.float32)
    scale = lax.rsqrt(jnp.sum(values * values, axis=-1, keepdims=True) + 1e-06)
    return (values * scale).astype(jnp.bfloat16)


def send(value, to):
    groups, members = lax.axis_size("grp"), lax.axis_size("blk")
    pairs = []
    for group in range(groups):
        for block in range(members):
            core = group % 2
            target = to(core, (block + core) % 2 == 1, block)
            if target is not None:
                pairs.append((group * members + block, group * members + target % members))
    return lax.ppermute(value, BOTH, pairs)


def params():
    return pltpu.CompilerParams(vmem_limit_bytes=56 * 1024 * 1024)


def vmem(n):
    return [pl.BlockSpec(memory_space=pltpu.VMEM)] * n


def smem():
    return [pl.BlockSpec(memory_space=pltpu.SMEM)]


def down(row):
    return jnp.broadcast_to(row, (128, row.shape[1])).T


def halves(numbers):
    numbers = numbers.astype(jnp.int32)
    return (numbers >> 7).astype(jnp.float32), (numbers & 127).astype(jnp.float32)


def numbers_of(ref):
    size = ref.shape[0] - EXTRA
    tail = ref[size:, :size].astype(jnp.float32)
    return (tail[0:1, :] * 128.0 + tail[1:2, :]).astype(jnp.int32)


def best(rows, row_ids, cols, col_down):
    scores = lax.dot_general(cols, rows, (((1,), (1,)), ((), ())), preferred_element_type=jnp.float32)
    found = []
    for left in range(0, rows.shape[0], 128):
        keep = col_down < row_ids[:, left : left + 128]
        part = jnp.where(keep, scores[:, left : left + 128], jnp.float32(LOWEST))
        found.append(jnp.max(part, axis=0, keepdims=True))
    return jnp.concatenate(found, axis=1)


def update(acc_ref, at_row, rows, cols):
    for _, col_ref in cols:
        size = col_ref.shape[0] - EXTRA
        col_down = down(numbers_of(col_ref))
        for half, row_ref in rows:
            row_ids = numbers_of(row_ref)
            for top in range(0, size, 256):
                found = best(row_ref[top : top + 256, :], row_ids[:, top : top + 256], col_ref[:size, :], col_down)
                at = slice(half * size + top, half * size + top + 256)
                acc_ref[at_row : at_row + 1, at] = jnp.maximum(acc_ref[at_row : at_row + 1, at], found)


def compare(where_ref, heavy, acc_ref, pairs):
    for core in (0, 1):

        @pl.when((where_ref[0] == core) & (where_ref[1] == heavy))
        def _():
            for (first, first_refs), (second, second_refs) in pairs:
                if core == 0:
                    update(acc_ref, first, first_refs, second_refs)
                else:
                    update(acc_ref, second, second_refs, first_refs)


def norm_kernel(x_ref, ids_ref, out_ref):
    size, width = x_ref.shape
    out_ref[:size, :] = normalize(x_ref[...])
    ids = jnp.concatenate([ids_ref[...], jnp.zeros((1, width - size), jnp.int32)], axis=1)
    high, low = halves(ids)
    row = lax.broadcasted_iota(jnp.int32, (EXTRA, width), 0)
    out_ref[size:, :] = jnp.where(row == 0, high, jnp.where(row == 1, low, 0.0)).astype(jnp.bfloat16)


def norm_half(embeds, ids, half):
    rows, width = embeds.shape
    size = rows // 2
    return pl.pallas_call(
        norm_kernel,
        grid=(1,),
        in_specs=[
            pl.BlockSpec((size, width), lambda i: (half, 0)),
            pl.BlockSpec((1, size), lambda i: (0, half)),
        ],
        out_specs=pl.BlockSpec((size + EXTRA, width), lambda i: (0, 0)),
        out_shape=jax.ShapeDtypeStruct((size + EXTRA, width), jnp.bfloat16),
        compiler_params=params(),
        name=f"norm_{half}",
        cost_estimate=pl.CostEstimate(flops=4 * size * width, bytes_accessed=4 * size * width, transcendentals=size),
    )(embeds, ids)


def place_kernel(rows_ref, target_ref, ids_ref, out_ref):
    count, width = rows_ref.shape
    target = target_ref[...]
    across = jnp.broadcast_to(target, (count, count))
    earlier = lax.broadcasted_iota(jnp.int32, (count, count), 0) < lax.broadcasted_iota(
        jnp.int32, (count, count), 1
    )
    same = (across.T == across) & earlier
    position = jnp.sum(same.astype(jnp.float32), axis=0, keepdims=True).astype(jnp.int32)
    place = target * CAP + position
    devices = out_ref.shape[0]
    slots = devices * CAP
    pick = (lax.broadcasted_iota(jnp.int32, (slots, count), 0) == place).astype(jnp.float32).astype(jnp.bfloat16)
    placed = jnp.dot(pick, normalize(rows_ref[...]), preferred_element_type=jnp.float32)
    out_ref[:, :, :width] = placed.astype(jnp.bfloat16).reshape(devices, CAP, width)
    high, low = halves(down(ids_ref[...]))
    lane = lax.broadcasted_iota(jnp.int32, high.shape, 1)
    pair = jnp.where(lane < 64, high + 1.0, low).astype(jnp.bfloat16)
    tail = jnp.dot(pick, pair, preferred_element_type=jnp.float32)
    out_ref[:, :, width:] = tail.astype(jnp.bfloat16).reshape(devices, CAP, 128)


def placed_rows(owned, target, ids, devices):
    count, width = owned.shape
    return pl.pallas_call(
        place_kernel,
        in_specs=vmem(3),
        out_specs=pl.BlockSpec(memory_space=pltpu.VMEM),
        out_shape=jax.ShapeDtypeStruct((devices, CAP, width + 128), jnp.bfloat16),
        compiler_params=params(),
        name="place",
        cost_estimate=pl.CostEstimate(
            flops=2 * devices * CAP * count * width, bytes_accessed=2 * (count + devices * CAP) * width, transcendentals=count
        ),
    )(owned, target, ids)


def split_kernel(in_ref, rows_ref, ids_ref):
    slots, width = rows_ref.shape
    rows_ref[...] = in_ref[:, :, :width].reshape(slots, width)
    tail = in_ref[:, :, width:].reshape(slots, 128).astype(jnp.float32).T
    high, low = tail[0:1, :], tail[64:65, :]
    ids_ref[...] = jnp.where(high == 0.0, -1.0, (high - 1.0) * 128.0 + low).astype(jnp.int32)


def split_rows(arrived):
    devices, cap, wide = arrived.shape
    slots, width = devices * cap, wide - 128
    return pl.pallas_call(
        split_kernel,
        in_specs=vmem(1),
        out_specs=vmem(2),
        out_shape=[
            jax.ShapeDtypeStruct((slots, width), jnp.bfloat16),
            jax.ShapeDtypeStruct((1, slots), jnp.int32),
        ],
        compiler_params=params(),
        name="split",
        cost_estimate=pl.CostEstimate(flops=0, bytes_accessed=4 * slots * width, transcendentals=0),
    )(arrived)


def within_kernel(own0, own1, prior_ref, acc_ref):
    acc_ref[...] = jnp.full(acc_ref.shape, LOWEST, jnp.float32)
    acc_ref[OWN : OWN + 1, :] = prior_ref[...]
    own = [(0, own0), (1, own1)]
    update(acc_ref, OWN, own, own)


def near_kernel(own0, own1, partner0, partner1, near0, near1, where_ref, so_far_ref, acc_ref):
    acc_ref[...] = so_far_ref[...]
    own = (OWN, [(0, own0), (1, own1)])
    partner = (PARTNER, [(0, partner0), (1, partner1)])
    near = (NEAR, [(0, near0), (1, near1)])
    compare(where_ref, 1, acc_ref, [(own, partner), (own, near), (partner, near)])
    compare(where_ref, 0, acc_ref, [(own, (NEAR_PARTNER, [(1, near1)]))])


def middle_kernel(
    own0, own1, partner0, partner1, near0, near1, near_partner0, far0, where_ref, so_far_ref, acc_ref, partner_out
):
    acc_ref[...] = so_far_ref[...]
    own = (OWN, [(0, own0), (1, own1)])
    partner = (PARTNER, [(0, partner0), (1, partner1)])
    near = (NEAR, [(0, near0), (1, near1)])
    near_partner = (NEAR_PARTNER, [(0, near_partner0)])
    far = (FAR_PARTNER, [(0, far0)])
    compare(where_ref, 1, acc_ref, [(own, near_partner), (partner, near_partner), (far, near)])
    partner_out[...] = acc_ref[PARTNER : PARTNER + 1, :]


def last_kernel(
    own0, own1, near0, near1, near_partner1, far1, where_ref, so_far_ref, own_out, far_out, side_out, acc_ref
):
    acc_ref[...] = so_far_ref[...]
    own = (OWN, [(0, own0), (1, own1)])
    near = (NEAR, [(0, near0), (1, near1)])
    near_partner = (NEAR_PARTNER, [(1, near_partner1)])
    far = (FAR_PARTNER, [(1, far1)])
    compare(where_ref, 1, acc_ref, [(own, near_partner), (far, near)])
    own_out[...] = acc_ref[OWN : OWN + 1, :]
    near_partner_row = acc_ref[NEAR_PARTNER : NEAR_PARTNER + 1, :]
    far_out[...] = jnp.where(where_ref[0] == 0, acc_ref[FAR_PARTNER : FAR_PARTNER + 1, :], near_partner_row)
    side_out[...] = jnp.where(where_ref[1] == 1, acc_ref[NEAR : NEAR + 1, :], near_partner_row)


def body(embeds, doc_ids, prior_max, owned, owned_ids, owner_dest):
    devices = lax.axis_size("grp") * lax.axis_size("blk")
    raw = embeds[0]
    rows, width = raw.shape
    core = lax.axis_index("grp") & 1
    heavy = (lax.axis_index("blk") + core) & 1
    where = jnp.stack([core, heavy]).astype(jnp.int32)

    def step(core):
        return 2 - 4 * core

    def to_heavy(core, heavy, block):
        return None if heavy else block ^ 1

    def to_light(core, heavy, block):
        return block ^ 1 if heavy else None

    def ahead(core, heavy, block):
        return block + step(core)

    def heavy_ahead(core, heavy, block):
        return block + step(core) if heavy else None

    def heavy_back(core, heavy, block):
        return block - step(core) if heavy else None

    own = [norm_half(raw, doc_ids, half) for half in range(2)]
    partner = [send(own[half], to_heavy) for half in range(2)]
    near1 = send(own[1], ahead)
    near0 = send(own[0], heavy_ahead)
    far = [send(partner[half], heavy_back) for half in range(2)]
    near_partner0 = send(partner[0], heavy_ahead)
    near_partner1 = send(near1, to_heavy)

    outgoing = placed_rows(owned, owner_dest.reshape(1, -1), owned_ids.reshape(1, -1), devices)
    next_rows, next_ids = split_rows(lax.all_to_all(outgoing, BOTH, split_axis=0, concat_axis=0, tiled=True))

    line = jax.ShapeDtypeStruct((1, rows), jnp.float32)
    acc = jax.ShapeDtypeStruct((8, rows), jnp.float32)

    def cost(products, blocks):
        return pl.CostEstimate(
            flops=int(2 * products * rows * rows * width), bytes_accessed=2 * blocks * rows * width, transcendentals=0
        )

    found = pl.pallas_call(
        within_kernel,
        in_specs=vmem(3),
        out_specs=pl.BlockSpec(memory_space=pltpu.VMEM),
        out_shape=acc,
        compiler_params=params(),
        name="within",
        cost_estimate=cost(1, 1),
    )(*own, prior_max)
    found = pl.pallas_call(
        near_kernel,
        in_specs=vmem(6) + smem() + vmem(1),
        out_specs=pl.BlockSpec(memory_space=pltpu.VMEM),
        out_shape=acc,
        compiler_params=params(),
        name="near",
        cost_estimate=cost(3, 3),
    )(*own, *partner, near0, near1, where, found)
    found, for_partner = pl.pallas_call(
        middle_kernel,
        in_specs=vmem(8) + smem() + vmem(1),
        out_specs=vmem(2),
        out_shape=[acc, line],
        compiler_params=params(),
        name="cross_middle",
        cost_estimate=cost(1.5, 4),
    )(*own, *partner, near0, near1, near_partner0, far[0], where, found)
    from_partner = send(for_partner, to_light)
    mine, for_far, for_side = pl.pallas_call(
        last_kernel,
        in_specs=vmem(6) + smem() + vmem(1),
        out_specs=vmem(3),
        out_shape=[line] * 3,
        scratch_shapes=[pltpu.VMEM((8, rows), jnp.float32)],
        compiler_params=params(),
        name="cross_last",
        cost_estimate=cost(1, 3),
    )(*own, near0, near1, near_partner1, far[1], where, found)
    from_far = send(for_far, lambda core, heavy, block: block + 1 + 2 * core if heavy else None)
    from_side = send(for_side, lambda core, heavy, block: block + 2 if core else None)
    lowest = jnp.float32(LOWEST)
    running = jnp.maximum(mine, jnp.where(heavy == 0, jnp.maximum(from_partner, from_far), lowest))
    running = jnp.maximum(running, jnp.where(core == 1, from_side, lowest))
    return (running, next_rows, next_ids.reshape(-1))


def solution(mesh):
    return jax.shard_map(
        body,
        mesh=mesh,
        in_specs=(
            P("grp", "blk", None),
            P("grp", "blk"),
            P("grp", "blk"),
            P(("grp", "blk"), None),
            P(("grp", "blk")),
            P(("grp", "blk"), None),
        ),
        out_specs=(P("grp", "blk"), P(("grp", "blk"), None), P(("grp", "blk"))),
        check_vma=False,
    )
```

```python
import jax
import jax.numpy as jnp
from jax import lax
from jax.experimental import pallas as pl
from jax.experimental.pallas import tpu as pltpu
from jax.sharding import PartitionSpec as P

CAP = 4
LOWEST = -2.0
EXTRA = 16
BOTH = ("grp", "blk")
OWN, PARTNER, NEAR, NEAR_PARTNER, FAR_PARTNER = range(5)


def normalize(matrix):
    values = matrix.astype(jnp.float32)
    scale = lax.rsqrt(jnp.sum(values * values, axis=-1, keepdims=True) + 1e-06)
    return (values * scale).astype(jnp.bfloat16)


def send(value, to):
    groups, members = lax.axis_size("grp"), lax.axis_size("blk")
    pairs = []
    for group in range(groups):
        for block in range(members):
            core = group % 2
            target = to(core, (block + core) % 2 == 1, block)
            if target is not None:
                pairs.append((group * members + block, group * members + target % members))
    return lax.ppermute(value, BOTH, pairs)


def params():
    return pltpu.CompilerParams(vmem_limit_bytes=24 * 1024 * 1024)


def vmem(n):
    return [pl.BlockSpec(memory_space=pltpu.VMEM)] * n


def smem():
    return [pl.BlockSpec(memory_space=pltpu.SMEM)]


def down(row):
    return jnp.broadcast_to(row, (128, row.shape[1])).T


def halves(numbers):
    numbers = numbers.astype(jnp.int32)
    return (numbers >> 7).astype(jnp.float32), (numbers & 127).astype(jnp.float32)


def numbers_of(ref):
    size = ref.shape[0] - EXTRA
    tail = ref[size:, :size].astype(jnp.float32)
    return (tail[0:1, :] * 128.0 + tail[1:2, :]).astype(jnp.int32)


def best(rows, row_ids, cols, col_down):
    scores = lax.dot_general(cols, rows, (((1,), (1,)), ((), ())), preferred_element_type=jnp.float32)
    found = []
    for left in range(0, rows.shape[0], 128):
        keep = col_down < row_ids[:, left : left + 128]
        part = jnp.where(keep, scores[:, left : left + 128], jnp.float32(LOWEST))
        found.append(jnp.max(part, axis=0, keepdims=True))
    return jnp.concatenate(found, axis=1)


def update(acc_ref, at_row, rows, cols):
    for _, col_ref in cols:
        size = col_ref.shape[0] - EXTRA
        col_down = down(numbers_of(col_ref))
        for half, row_ref in rows:
            row_ids = numbers_of(row_ref)
            for top in range(0, size, 256):
                found = best(row_ref[top : top + 256, :], row_ids[:, top : top + 256], col_ref[:size, :], col_down)
                at = slice(half * size + top, half * size + top + 256)
                acc_ref[at_row : at_row + 1, at] = jnp.maximum(acc_ref[at_row : at_row + 1, at], found)


def compare(where_ref, heavy, acc_ref, pairs):
    for core in (0, 1):

        @pl.when((where_ref[0] == core) & (where_ref[1] == heavy))
        def _():
            for (first, first_refs), (second, second_refs) in pairs:
                if core == 0:
                    update(acc_ref, first, first_refs, second_refs)
                else:
                    update(acc_ref, second, second_refs, first_refs)


def norm_kernel(x_ref, ids_ref, out_ref):
    size, width = x_ref.shape
    out_ref[:size, :] = normalize(x_ref[...])
    ids = jnp.concatenate([ids_ref[...], jnp.zeros((1, width - size), jnp.int32)], axis=1)
    high, low = halves(ids)
    row = lax.broadcasted_iota(jnp.int32, (EXTRA, width), 0)
    out_ref[size:, :] = jnp.where(row == 0, high, jnp.where(row == 1, low, 0.0)).astype(jnp.bfloat16)


def norm_half(embeds, ids, half):
    rows, width = embeds.shape
    size = rows // 2
    return pl.pallas_call(
        norm_kernel,
        grid=(1,),
        in_specs=[
            pl.BlockSpec((size, width), lambda i: (half, 0)),
            pl.BlockSpec((1, size), lambda i: (0, half)),
        ],
        out_specs=pl.BlockSpec((size + EXTRA, width), lambda i: (0, 0)),
        out_shape=jax.ShapeDtypeStruct((size + EXTRA, width), jnp.bfloat16),
        compiler_params=params(),
        name=f"norm_{half}",
        cost_estimate=pl.CostEstimate(flops=4 * size * width, bytes_accessed=4 * size * width, transcendentals=size),
    )(embeds, ids)


def place_kernel(rows_ref, target_ref, ids_ref, out_ref):
    count, width = rows_ref.shape
    target = target_ref[...]
    across = jnp.broadcast_to(target, (count, count))
    earlier = lax.broadcasted_iota(jnp.int32, (count, count), 0) < lax.broadcasted_iota(
        jnp.int32, (count, count), 1
    )
    same = (across.T == across) & earlier
    position = jnp.sum(same.astype(jnp.float32), axis=0, keepdims=True).astype(jnp.int32)
    place = target * CAP + position
    devices = out_ref.shape[0]
    slots = devices * CAP
    pick = (lax.broadcasted_iota(jnp.int32, (slots, count), 0) == place).astype(jnp.float32).astype(jnp.bfloat16)
    placed = jnp.dot(pick, normalize(rows_ref[...]), preferred_element_type=jnp.float32)
    out_ref[:, :, :width] = placed.astype(jnp.bfloat16).reshape(devices, CAP, width)
    high, low = halves(down(ids_ref[...]))
    lane = lax.broadcasted_iota(jnp.int32, high.shape, 1)
    pair = jnp.where(lane < 64, high + 1.0, low).astype(jnp.bfloat16)
    tail = jnp.dot(pick, pair, preferred_element_type=jnp.float32)
    out_ref[:, :, width:] = tail.astype(jnp.bfloat16).reshape(devices, CAP, 128)


def placed_rows(owned, target, ids, devices):
    count, width = owned.shape
    return pl.pallas_call(
        place_kernel,
        in_specs=vmem(3),
        out_specs=pl.BlockSpec(memory_space=pltpu.VMEM),
        out_shape=jax.ShapeDtypeStruct((devices, CAP, width + 128), jnp.bfloat16),
        compiler_params=params(),
        name="place",
        cost_estimate=pl.CostEstimate(
            flops=2 * devices * CAP * count * width, bytes_accessed=2 * (count + devices * CAP) * width, transcendentals=count
        ),
    )(owned, target, ids)


def split_kernel(in_ref, rows_ref, ids_ref):
    slots, width = rows_ref.shape
    rows_ref[...] = in_ref[:, :, :width].reshape(slots, width)
    tail = in_ref[:, :, width:].reshape(slots, 128).astype(jnp.float32).T
    high, low = tail[0:1, :], tail[64:65, :]
    ids_ref[...] = jnp.where(high == 0.0, -1.0, (high - 1.0) * 128.0 + low).astype(jnp.int32)


def split_rows(arrived):
    devices, cap, wide = arrived.shape
    slots, width = devices * cap, wide - 128
    return pl.pallas_call(
        split_kernel,
        in_specs=vmem(1),
        out_specs=vmem(2),
        out_shape=[
            jax.ShapeDtypeStruct((slots, width), jnp.bfloat16),
            jax.ShapeDtypeStruct((1, slots), jnp.int32),
        ],
        compiler_params=params(),
        name="split",
        cost_estimate=pl.CostEstimate(flops=0, bytes_accessed=4 * slots * width, transcendentals=0),
    )(arrived)


def within_kernel(own0, own1, prior_ref, acc_ref):
    acc_ref[...] = jnp.full(acc_ref.shape, LOWEST, jnp.float32)
    acc_ref[OWN : OWN + 1, :] = prior_ref[...]
    own = [(0, own0), (1, own1)]
    update(acc_ref, OWN, own, own)


def near_kernel(own0, own1, partner0, partner1, near0, near1, where_ref, so_far_ref, after_ref, acc_ref):
    del after_ref
    acc_ref[...] = so_far_ref[...]
    own = (OWN, [(0, own0), (1, own1)])
    partner = (PARTNER, [(0, partner0), (1, partner1)])
    near = (NEAR, [(0, near0), (1, near1)])
    compare(where_ref, 1, acc_ref, [(own, partner), (own, near), (partner, near)])
    compare(where_ref, 0, acc_ref, [(own, (NEAR_PARTNER, [(1, near1)]))])


def middle_kernel(
    own0, own1, partner0, partner1, near0, near1, near_partner0, far0, where_ref, so_far_ref, acc_ref, partner_out
):
    acc_ref[...] = so_far_ref[...]
    own = (OWN, [(0, own0), (1, own1)])
    partner = (PARTNER, [(0, partner0), (1, partner1)])
    near = (NEAR, [(0, near0), (1, near1)])
    near_partner = (NEAR_PARTNER, [(0, near_partner0)])
    far = (FAR_PARTNER, [(0, far0)])
    compare(where_ref, 1, acc_ref, [(own, near_partner), (partner, near_partner), (far, near)])
    partner_out[...] = acc_ref[PARTNER : PARTNER + 1, :]


def last_kernel(
    own0, own1, near0, near1, near_partner1, far1, where_ref, so_far_ref, from_partner_ref, own_out, far_out, side_out, acc_ref
):
    acc_ref[...] = so_far_ref[...]
    own = (OWN, [(0, own0), (1, own1)])
    near = (NEAR, [(0, near0), (1, near1)])
    near_partner = (NEAR_PARTNER, [(1, near_partner1)])
    far = (FAR_PARTNER, [(1, far1)])
    compare(where_ref, 1, acc_ref, [(own, near_partner), (far, near)])
    own_row = acc_ref[OWN : OWN + 1, :]
    own_out[...] = jnp.where(where_ref[1] == 0, jnp.maximum(own_row, from_partner_ref[...]), own_row)
    near_partner_row = acc_ref[NEAR_PARTNER : NEAR_PARTNER + 1, :]
    far_out[...] = jnp.where(where_ref[0] == 0, acc_ref[FAR_PARTNER : FAR_PARTNER + 1, :], near_partner_row)
    side_out[...] = jnp.where(where_ref[1] == 1, acc_ref[NEAR : NEAR + 1, :], near_partner_row)


def body(embeds, doc_ids, prior_max, owned, owned_ids, owner_dest):
    devices = lax.axis_size("grp") * lax.axis_size("blk")
    raw = embeds[0]
    rows, width = raw.shape
    core = lax.axis_index("grp") & 1
    heavy = (lax.axis_index("blk") + core) & 1
    where = jnp.stack([core, heavy]).astype(jnp.int32)

    def step(core):
        return 2 - 4 * core

    def to_heavy(core, heavy, block):
        return None if heavy else block ^ 1

    def to_light(core, heavy, block):
        return block ^ 1 if heavy else None

    def ahead(core, heavy, block):
        return block + step(core)

    def heavy_ahead(core, heavy, block):
        return block + step(core) if heavy else None

    def heavy_back(core, heavy, block):
        return block - step(core) if heavy else None

    own = [norm_half(raw, doc_ids, half) for half in range(2)]
    partner = [send(own[half], to_heavy) for half in range(2)]
    near1 = send(own[1], ahead)
    near0 = send(own[0], heavy_ahead)
    far = [send(partner[half], heavy_back) for half in range(2)]
    near_partner0 = send(partner[0], heavy_ahead)
    near_partner1 = send(near1, to_heavy)

    outgoing = placed_rows(owned, owner_dest.reshape(1, -1), owned_ids.reshape(1, -1), devices)
    next_rows, next_ids = split_rows(lax.all_to_all(outgoing, BOTH, split_axis=0, concat_axis=0, tiled=True))

    line = jax.ShapeDtypeStruct((1, rows), jnp.float32)
    acc = jax.ShapeDtypeStruct((8, rows), jnp.float32)

    def cost(products, blocks):
        return pl.CostEstimate(
            flops=int(2 * products * rows * rows * width), bytes_accessed=2 * blocks * rows * width, transcendentals=0
        )

    found = pl.pallas_call(
        within_kernel,
        in_specs=vmem(3),
        out_specs=pl.BlockSpec(memory_space=pltpu.VMEM),
        out_shape=acc,
        compiler_params=params(),
        name="within",
        cost_estimate=cost(1, 1),
    )(*own, prior_max)
    found = pl.pallas_call(
        near_kernel,
        in_specs=vmem(6) + smem() + vmem(1) + [pl.BlockSpec(memory_space=pl.ANY)],
        out_specs=pl.BlockSpec(memory_space=pltpu.VMEM),
        out_shape=acc,
        compiler_params=params(),
        name="near",
        cost_estimate=cost(3, 3),
    )(*own, *partner, near0, near1, where, found, next_ids)
    found, for_partner = pl.pallas_call(
        middle_kernel,
        in_specs=vmem(8) + smem() + vmem(1),
        out_specs=vmem(2),
        out_shape=[acc, line],
        compiler_params=params(),
        name="cross_middle",
        cost_estimate=cost(1.5, 4),
    )(*own, *partner, near0, near1, near_partner0, far[0], where, found)
    from_partner = send(for_partner, to_light)
    mine, for_far, for_side = pl.pallas_call(
        last_kernel,
        in_specs=vmem(6) + smem() + vmem(2),
        out_specs=vmem(3),
        out_shape=[line] * 3,
        scratch_shapes=[pltpu.VMEM((8, rows), jnp.float32)],
        compiler_params=params(),
        name="cross_last",
        cost_estimate=cost(1, 3),
    )(*own, near0, near1, near_partner1, far[1], where, found, from_partner)
    from_far = send(for_far, lambda core, heavy, block: block + 1 + 2 * core if heavy else None)
    from_side = send(for_side, lambda core, heavy, block: block + 2 if core else None)
    lowest = jnp.float32(LOWEST)
    running = jnp.maximum(mine, jnp.where(heavy == 0, from_far, lowest))
    running = jnp.maximum(running, jnp.where(core == 1, from_side, lowest))
    return (running, next_rows, next_ids.reshape(-1))


def solution(mesh):
    return jax.shard_map(
        body,
        mesh=mesh,
        in_specs=(
            P("grp", "blk", None),
            P("grp", "blk"),
            P("grp", "blk"),
            P(("grp", "blk"), None),
            P(("grp", "blk")),
            P(("grp", "blk"), None),
        ),
        out_specs=(P("grp", "blk"), P(("grp", "blk"), None), P(("grp", "blk"))),
        check_vma=False,
    )
```

```python
import jax
import jax.numpy as jnp
from jax import lax
from jax.experimental import pallas as pl
from jax.experimental.pallas import tpu as pltpu
from jax.sharding import PartitionSpec as P

CAP = 4
LOWEST = -2.0
EXTRA = 16
TIES = True
BOTH = ("grp", "blk")
OWN, PARTNER, NEAR, NEAR_PARTNER, FAR_PARTNER = range(5)


def normalize(matrix):
    values = matrix.astype(jnp.float32)
    scale = lax.rsqrt(jnp.sum(values * values, axis=-1, keepdims=True) + 1e-06)
    return (values * scale).astype(jnp.bfloat16)


def send(value, to):
    groups, members = lax.axis_size("grp"), lax.axis_size("blk")
    pairs = []
    for group in range(groups):
        for block in range(members):
            core = group % 2
            target = to(core, (block + core) % 2 == 1, block)
            if target is not None:
                pairs.append((group * members + block, group * members + target % members))
    return lax.ppermute(value, BOTH, pairs)


def params():
    return pltpu.CompilerParams(vmem_limit_bytes=24 * 1024 * 1024)


def vmem(n):
    return [pl.BlockSpec(memory_space=pltpu.VMEM)] * n


def smem():
    return [pl.BlockSpec(memory_space=pltpu.SMEM)]


def down(row):
    return jnp.broadcast_to(row, (128, row.shape[1])).T


def halves(numbers):
    numbers = numbers.astype(jnp.int32)
    return (numbers >> 7).astype(jnp.float32), (numbers & 127).astype(jnp.float32)


def numbers_of(ref):
    size = ref.shape[0] - EXTRA
    tail = ref[size:, :size].astype(jnp.float32)
    return (tail[0:1, :] * 128.0 + tail[1:2, :]).astype(jnp.int32)


def best(rows, row_ids, cols, col_down):
    scores = lax.dot_general(cols, rows, (((1,), (1,)), ((), ())), preferred_element_type=jnp.float32)
    found = []
    for left in range(0, rows.shape[0], 128):
        keep = col_down < row_ids[:, left : left + 128]
        part = jnp.where(keep, scores[:, left : left + 128], jnp.float32(LOWEST))
        found.append(jnp.max(part, axis=0, keepdims=True))
    return jnp.concatenate(found, axis=1)


def update(acc_ref, at_row, rows, cols, arrive):
    for _, col in cols:
        col_ref = arrive(col)
        size = col_ref.shape[0] - EXTRA
        col_down = down(numbers_of(col_ref))
        for half, row in rows:
            row_ref = arrive(row)
            row_ids = numbers_of(row_ref)
            for top in range(0, size, 256):
                found = best(row_ref[top : top + 256, :], row_ids[:, top : top + 256], col_ref[:size, :], col_down)
                at = slice(half * size + top, half * size + top + 256)
                acc_ref[at_row : at_row + 1, at] = jnp.maximum(acc_ref[at_row : at_row + 1, at], found)


def compare(where_ref, heavy, acc_ref, names, refs, buffers, sems, pairs):
    needed = [name for name in names if any(name == n for p in pairs for side in p for _, n in side[1])]

    def run(core):
        copies = {
            name: pltpu.make_async_copy(refs[names.index(name)], buffers.at[k], sems.at[k])
            for k, name in enumerate(needed)
        }
        for copy in copies.values():
            copy.start()
        there = set()

        def arrive(name):
            if name not in there:
                copies[name].wait()
                there.add(name)
            return buffers.at[needed.index(name)]

        for (first, first_halves), (second, second_halves) in pairs:
            if core == 0:
                update(acc_ref, first, first_halves, second_halves, arrive)
            else:
                update(acc_ref, second, second_halves, first_halves, arrive)

    for core in (0, 1):

        @pl.when((where_ref[0] == core) & (where_ref[1] == heavy))
        def _():
            run(core)


def norm_kernel(x_ref, ids_ref, out_ref):
    size, width = x_ref.shape
    out_ref[:size, :] = normalize(x_ref[...])
    ids = jnp.concatenate([ids_ref[...], jnp.zeros((1, width - size), jnp.int32)], axis=1)
    high, low = halves(ids)
    row = lax.broadcasted_iota(jnp.int32, (EXTRA, width), 0)
    out_ref[size:, :] = jnp.where(row == 0, high, jnp.where(row == 1, low, 0.0)).astype(jnp.bfloat16)


def norm_half(embeds, ids, half):
    rows, width = embeds.shape
    size = rows // 2
    return pl.pallas_call(
        norm_kernel,
        grid=(1,),
        in_specs=[
            pl.BlockSpec((size, width), lambda i: (half, 0)),
            pl.BlockSpec((1, size), lambda i: (0, half)),
        ],
        out_specs=pl.BlockSpec((size + EXTRA, width), lambda i: (0, 0)),
        out_shape=jax.ShapeDtypeStruct((size + EXTRA, width), jnp.bfloat16),
        compiler_params=params(),
        name=f"norm_{half}",
        cost_estimate=pl.CostEstimate(flops=4 * size * width, bytes_accessed=4 * size * width, transcendentals=size),
    )(embeds, ids)


def place_kernel(rows_ref, target_ref, ids_ref, out_ref):
    count, width = rows_ref.shape
    target = target_ref[...]
    across = jnp.broadcast_to(target, (count, count))
    earlier = lax.broadcasted_iota(jnp.int32, (count, count), 0) < lax.broadcasted_iota(
        jnp.int32, (count, count), 1
    )
    same = (across.T == across) & earlier
    position = jnp.sum(same.astype(jnp.float32), axis=0, keepdims=True).astype(jnp.int32)
    place = target * CAP + position
    devices = out_ref.shape[0]
    slots = devices * CAP
    pick = (lax.broadcasted_iota(jnp.int32, (slots, count), 0) == place).astype(jnp.float32).astype(jnp.bfloat16)
    placed = jnp.dot(pick, normalize(rows_ref[...]), preferred_element_type=jnp.float32)
    out_ref[:, :, :width] = placed.astype(jnp.bfloat16).reshape(devices, CAP, width)
    high, low = halves(down(ids_ref[...]))
    lane = lax.broadcasted_iota(jnp.int32, high.shape, 1)
    pair = jnp.where(lane < 64, high + 1.0, low).astype(jnp.bfloat16)
    tail = jnp.dot(pick, pair, preferred_element_type=jnp.float32)
    out_ref[:, :, width:] = tail.astype(jnp.bfloat16).reshape(devices, CAP, 128)


def placed_rows(owned, target, ids, devices):
    count, width = owned.shape
    return pl.pallas_call(
        place_kernel,
        in_specs=vmem(3),
        out_specs=pl.BlockSpec(memory_space=pltpu.VMEM),
        out_shape=jax.ShapeDtypeStruct((devices, CAP, width + 128), jnp.bfloat16),
        compiler_params=params(),
        name="place",
        cost_estimate=pl.CostEstimate(
            flops=2 * devices * CAP * count * width, bytes_accessed=2 * (count + devices * CAP) * width, transcendentals=count
        ),
    )(owned, target, ids)


def split_kernel(in_ref, rows_ref, ids_ref):
    slots, width = rows_ref.shape
    rows_ref[...] = in_ref[:, :, :width].reshape(slots, width)
    tail = in_ref[:, :, width:].reshape(slots, 128).astype(jnp.float32).T
    high, low = tail[0:1, :], tail[64:65, :]
    ids_ref[...] = jnp.where(high == 0.0, -1.0, (high - 1.0) * 128.0 + low).astype(jnp.int32)


def split_rows(arrived):
    devices, cap, wide = arrived.shape
    slots, width = devices * cap, wide - 128
    return pl.pallas_call(
        split_kernel,
        in_specs=vmem(1),
        out_specs=vmem(2),
        out_shape=[
            jax.ShapeDtypeStruct((slots, width), jnp.bfloat16),
            jax.ShapeDtypeStruct((1, slots), jnp.int32),
        ],
        compiler_params=params(),
        name="split",
        cost_estimate=pl.CostEstimate(flops=20 * 10**9, bytes_accessed=4 * slots * width, transcendentals=0),
    )(arrived)


def within_kernel(own0, own1, prior_ref, acc_ref):
    acc_ref[...] = jnp.full(acc_ref.shape, LOWEST, jnp.float32)
    acc_ref[OWN : OWN + 1, :] = prior_ref[...]
    own = [(0, 0), (1, 1)]
    update(acc_ref, OWN, own, own, lambda half: (own0, own1)[half])


def stage(name, arrays, heavy_pairs, light_pairs, where, found, after=()):
    names = list(arrays)
    size, width = arrays[names[0]].shape
    rows = found.shape[1]

    def run(*refs):
        inputs, where_ref, so_far_ref = refs[: len(names)], refs[len(names)], refs[len(names) + 1]
        acc_ref, buffers, sems = refs[-3:]
        acc_ref[...] = so_far_ref[...]
        compare(where_ref, 1, acc_ref, names, inputs, buffers, sems, heavy_pairs)
        if light_pairs:
            compare(where_ref, 0, acc_ref, names, inputs, buffers, sems, light_pairs)

    products = sum(len(a[1]) * len(b[1]) for a, b in heavy_pairs) / 4
    return pl.pallas_call(
        run,
        in_specs=[pl.BlockSpec(memory_space=pltpu.HBM)] * len(names)
        + smem()
        + vmem(1)
        + vmem(len(after)),
        out_specs=pl.BlockSpec(memory_space=pltpu.VMEM),
        out_shape=jax.ShapeDtypeStruct(found.shape, jnp.float32),
        scratch_shapes=[pltpu.VMEM((len(names), size, width), jnp.bfloat16), pltpu.SemaphoreType.DMA((len(names),))],
        compiler_params=params(),
        name=name,
        cost_estimate=pl.CostEstimate(
            flops=int(2 * products * rows * rows * width),
            bytes_accessed=2 * len(names) * size * width,
            transcendentals=0,
        ),
    )(*arrays.values(), where, found, *after)


def tie_kernel(array_ref, after_ref, out_ref):
    del array_ref, after_ref, out_ref


def tie(array, after):
    return pl.pallas_call(
        tie_kernel,
        in_specs=[pl.BlockSpec(memory_space=pltpu.HBM)] + vmem(1),
        out_specs=pl.BlockSpec(memory_space=pltpu.HBM),
        out_shape=jax.ShapeDtypeStruct(array.shape, array.dtype),
        input_output_aliases={0: 0},
        compiler_params=params(),
        name="tie",
        cost_estimate=pl.CostEstimate(flops=0, bytes_accessed=0, transcendentals=0),
    )(array, after)


def results_kernel(where_ref, so_far_ref, from_partner_ref, own_out, far_out, side_out):
    own_row = so_far_ref[OWN : OWN + 1, :]
    own_out[...] = jnp.where(where_ref[1] == 0, jnp.maximum(own_row, from_partner_ref[...]), own_row)
    near_partner_row = so_far_ref[NEAR_PARTNER : NEAR_PARTNER + 1, :]
    far_out[...] = jnp.where(where_ref[0] == 0, so_far_ref[FAR_PARTNER : FAR_PARTNER + 1, :], near_partner_row)
    side_out[...] = jnp.where(where_ref[1] == 1, so_far_ref[NEAR : NEAR + 1, :], near_partner_row)


def body(embeds, doc_ids, prior_max, owned, owned_ids, owner_dest):
    devices = lax.axis_size("grp") * lax.axis_size("blk")
    raw = embeds[0]
    rows, width = raw.shape
    core = lax.axis_index("grp") & 1
    heavy = (lax.axis_index("blk") + core) & 1
    where = jnp.stack([core, heavy]).astype(jnp.int32)

    def step(core):
        return 2 - 4 * core

    def to_heavy(core, heavy, block):
        return None if heavy else block ^ 1

    def to_light(core, heavy, block):
        return block ^ 1 if heavy else None

    def ahead(core, heavy, block):
        return block + step(core)

    def heavy_ahead(core, heavy, block):
        return block + step(core) if heavy else None

    def heavy_back(core, heavy, block):
        return block - step(core) if heavy else None

    outgoing = placed_rows(owned, owner_dest.reshape(1, -1), owned_ids.reshape(1, -1), devices)
    next_rows, next_ids = split_rows(lax.all_to_all(outgoing, BOTH, split_axis=0, concat_axis=0, tiled=True))

    line = jax.ShapeDtypeStruct((1, rows), jnp.float32)
    own0, own1 = (norm_half(raw, doc_ids, half) for half in range(2))
    partner0 = send(own0, to_heavy)
    near1 = send(own1, ahead)
    partner1 = send(own1, to_heavy)
    near0 = send(own0, heavy_ahead)

    found = pl.pallas_call(
        within_kernel,
        in_specs=vmem(3),
        out_specs=pl.BlockSpec(memory_space=pltpu.VMEM),
        out_shape=jax.ShapeDtypeStruct((8, rows), jnp.float32),
        compiler_params=params(),
        name="within",
        cost_estimate=pl.CostEstimate(
            flops=2 * rows * rows * width, bytes_accessed=2 * rows * width, transcendentals=0
        ),
    )(own0, own1, prior_max)
    if TIES:
        partner0 = tie(partner0, found)
    far0 = send(partner0, heavy_back)
    near_partner0 = send(partner0, heavy_ahead)
    near_partner1 = send(near1, to_heavy)

    own = (OWN, [(0, "own0"), (1, "own1")])
    found = stage(
        "cross_a",
        {"own0": own0, "own1": own1, "partner0": partner0, "near1": near1},
        [
            (own, (PARTNER, [(0, "partner0")])),
            (own, (NEAR, [(1, "near1")])),
            ((PARTNER, [(0, "partner0")]), (NEAR, [(1, "near1")])),
        ],
        [(own, (NEAR_PARTNER, [(1, "near1")]))],
        where,
        found,
        (next_ids,),
    )
    if TIES:
        partner1 = tie(partner1, found)
    far1 = send(partner1, heavy_back)
    found = stage(
        "cross_b",
        {"own0": own0, "own1": own1, "partner1": partner1, "near0": near0, "partner0": partner0, "near1": near1},
        [
            (own, (PARTNER, [(1, "partner1")])),
            (own, (NEAR, [(0, "near0")])),
            ((PARTNER, [(0, "partner0"), (1, "partner1")]), (NEAR, [(0, "near0")])),
            ((PARTNER, [(1, "partner1")]), (NEAR, [(1, "near1")])),
        ],
        [],
        where,
        found,
    )
    near_both = (NEAR, [(0, "near0"), (1, "near1")])
    found = stage(
        "cross_c",
        {
            "own0": own0,
            "near_partner0": near_partner0,
            "own1": own1,
            "partner0": partner0,
            "partner1": partner1,
            "near0": near0,
            "far0": far0,
            "near1": near1,
        },
        [
            (own, (NEAR_PARTNER, [(0, "near_partner0")])),
            ((PARTNER, [(0, "partner0"), (1, "partner1")]), (NEAR_PARTNER, [(0, "near_partner0")])),
            ((FAR_PARTNER, [(0, "far0")]), near_both),
        ],
        [],
        where,
        found,
    )
    from_partner = send(found[PARTNER : PARTNER + 1], to_light)
    found = stage(
        "cross_d",
        {
            "own0": own0,
            "near_partner1": near_partner1,
            "own1": own1,
            "near0": near0,
            "far1": far1,
            "near1": near1,
        },
        [
            (own, (NEAR_PARTNER, [(1, "near_partner1")])),
            ((FAR_PARTNER, [(1, "far1")]), near_both),
        ],
        [],
        where,
        found,
    )
    mine, for_far, for_side = pl.pallas_call(
        results_kernel,
        in_specs=smem() + vmem(2),
        out_specs=vmem(3),
        out_shape=[line] * 3,
        compiler_params=params(),
        name="results",
    )(where, found, from_partner)
    from_far = send(for_far, lambda core, heavy, block: block + 1 + 2 * core if heavy else None)
    from_side = send(for_side, lambda core, heavy, block: block + 2 if core else None)
    lowest = jnp.float32(LOWEST)
    running = jnp.maximum(mine, jnp.where(heavy == 0, from_far, lowest))
    running = jnp.maximum(running, jnp.where(core == 1, from_side, lowest))
    return (running, next_rows, next_ids.reshape(-1))


def solution(mesh):
    return jax.shard_map(
        body,
        mesh=mesh,
        in_specs=(
            P("grp", "blk", None),
            P("grp", "blk"),
            P("grp", "blk"),
            P(("grp", "blk"), None),
            P(("grp", "blk")),
            P(("grp", "blk"), None),
        ),
        out_specs=(P("grp", "blk"), P(("grp", "blk"), None), P(("grp", "blk"))),
        check_vma=False,
    )
```

```python
import jax
import jax.numpy as jnp
from jax import lax
from jax.experimental import pallas as pl
from jax.experimental.pallas import tpu as pltpu
from jax.sharding import PartitionSpec as P

CAP = 4
LOWEST = -2.0
EXTRA = 16
AHEAD = 1
BOTH = ("grp", "blk")
OWN, PARTNER, NEAR, NEAR_PARTNER, FAR_PARTNER = range(5)


def normalize(matrix):
    values = matrix.astype(jnp.float32)
    scale = lax.rsqrt(jnp.sum(values * values, axis=-1, keepdims=True) + 1e-06)
    return (values * scale).astype(jnp.bfloat16)


def send(value, to):
    groups, members = lax.axis_size("grp"), lax.axis_size("blk")
    pairs = []
    for group in range(groups):
        for block in range(members):
            core = group % 2
            target = to(core, (block + core) % 2 == 1, block)
            if target is not None:
                pairs.append((group * members + block, group * members + target % members))
    return lax.ppermute(value, BOTH, pairs)


def params():
    return pltpu.CompilerParams(vmem_limit_bytes=24 * 1024 * 1024)


def vmem(n):
    return [pl.BlockSpec(memory_space=pltpu.VMEM)] * n


def smem():
    return [pl.BlockSpec(memory_space=pltpu.SMEM)]


def down(row):
    return jnp.broadcast_to(row, (128, row.shape[1])).T


def halves(numbers):
    numbers = numbers.astype(jnp.int32)
    return (numbers >> 7).astype(jnp.float32), (numbers & 127).astype(jnp.float32)


def numbers_of(ref):
    size = ref.shape[0] - EXTRA
    tail = ref[size:, :size].astype(jnp.float32)
    return (tail[0:1, :] * 128.0 + tail[1:2, :]).astype(jnp.int32)


def best(rows, row_ids, cols, col_down):
    scores = lax.dot_general(cols, rows, (((1,), (1,)), ((), ())), preferred_element_type=jnp.float32)
    found = []
    for left in range(0, rows.shape[0], 128):
        keep = col_down < row_ids[:, left : left + 128]
        part = jnp.where(keep, scores[:, left : left + 128], jnp.float32(LOWEST))
        found.append(jnp.max(part, axis=0, keepdims=True))
    return jnp.concatenate(found, axis=1)


def update(acc_ref, at_row, rows, cols, arrive):
    for _, col in cols:
        col_ref = arrive(col)
        size = col_ref.shape[0] - EXTRA
        col_down = down(numbers_of(col_ref))
        for half, row in rows:
            row_ref = arrive(row)
            row_ids = numbers_of(row_ref)
            for top in range(0, size, 256):
                found = best(row_ref[top : top + 256, :], row_ids[:, top : top + 256], col_ref[:size, :], col_down)
                at = slice(half * size + top, half * size + top + 256)
                acc_ref[at_row : at_row + 1, at] = jnp.maximum(acc_ref[at_row : at_row + 1, at], found)


def compare(where_ref, heavy, acc_ref, held, names, refs, buffers, sems, pairs):
    needed = [name for name in names if any(name == n for p in pairs for side in p for _, n in side[1])]

    def run(core):
        copies = {
            name: pltpu.make_async_copy(refs[names.index(name)], buffers.at[k], sems.at[k])
            for k, name in enumerate(needed)
        }
        started, there = set(), set()

        def arrive(name):
            if name in held:
                return held[name]
            if name not in there:
                for k, other in enumerate(needed):
                    if other not in started and k <= needed.index(name) + AHEAD:
                        copies[other].start()
                        started.add(other)
                copies[name].wait()
                there.add(name)
            return buffers.at[needed.index(name)]

        for (first, first_halves), (second, second_halves) in pairs:
            if core == 0:
                update(acc_ref, first, first_halves, second_halves, arrive)
            else:
                update(acc_ref, second, second_halves, first_halves, arrive)

    for core in (0, 1):

        @pl.when((where_ref[0] == core) & (where_ref[1] == heavy))
        def _():
            run(core)


def norm_kernel(x_ref, ids_ref, out_ref):
    size, width = x_ref.shape
    out_ref[:size, :] = normalize(x_ref[...])
    ids = jnp.concatenate([ids_ref[...], jnp.zeros((1, width - size), jnp.int32)], axis=1)
    high, low = halves(ids)
    row = lax.broadcasted_iota(jnp.int32, (EXTRA, width), 0)
    out_ref[size:, :] = jnp.where(row == 0, high, jnp.where(row == 1, low, 0.0)).astype(jnp.bfloat16)


def norm_half(embeds, ids, half):
    rows, width = embeds.shape
    size = rows // 2
    return pl.pallas_call(
        norm_kernel,
        grid=(1,),
        in_specs=[
            pl.BlockSpec((size, width), lambda i: (half, 0)),
            pl.BlockSpec((1, size), lambda i: (0, half)),
        ],
        out_specs=pl.BlockSpec((size + EXTRA, width), lambda i: (0, 0)),
        out_shape=jax.ShapeDtypeStruct((size + EXTRA, width), jnp.bfloat16),
        compiler_params=params(),
        name=f"norm_{half}",
        cost_estimate=pl.CostEstimate(flops=4 * size * width, bytes_accessed=4 * size * width, transcendentals=size),
    )(embeds, ids)


def place_kernel(rows_ref, target_ref, ids_ref, out_ref):
    count, width = rows_ref.shape
    target = target_ref[...]
    across = jnp.broadcast_to(target, (count, count))
    earlier = lax.broadcasted_iota(jnp.int32, (count, count), 0) < lax.broadcasted_iota(
        jnp.int32, (count, count), 1
    )
    same = (across.T == across) & earlier
    position = jnp.sum(same.astype(jnp.float32), axis=0, keepdims=True).astype(jnp.int32)
    place = target * CAP + position
    devices = out_ref.shape[0]
    slots = devices * CAP
    pick = (lax.broadcasted_iota(jnp.int32, (slots, count), 0) == place).astype(jnp.float32).astype(jnp.bfloat16)
    placed = jnp.dot(pick, normalize(rows_ref[...]), preferred_element_type=jnp.float32)
    out_ref[:, :, :width] = placed.astype(jnp.bfloat16).reshape(devices, CAP, width)
    high, low = halves(down(ids_ref[...]))
    lane = lax.broadcasted_iota(jnp.int32, high.shape, 1)
    pair = jnp.where(lane < 64, high + 1.0, low).astype(jnp.bfloat16)
    tail = jnp.dot(pick, pair, preferred_element_type=jnp.float32)
    out_ref[:, :, width:] = tail.astype(jnp.bfloat16).reshape(devices, CAP, 128)


def placed_rows(owned, target, ids, devices):
    count, width = owned.shape
    return pl.pallas_call(
        place_kernel,
        in_specs=vmem(3),
        out_specs=pl.BlockSpec(memory_space=pltpu.VMEM),
        out_shape=jax.ShapeDtypeStruct((devices, CAP, width + 128), jnp.bfloat16),
        compiler_params=params(),
        name="place",
        cost_estimate=pl.CostEstimate(
            flops=2 * devices * CAP * count * width, bytes_accessed=2 * (count + devices * CAP) * width, transcendentals=count
        ),
    )(owned, target, ids)


def split_kernel(in_ref, rows_ref, ids_ref):
    slots, width = rows_ref.shape
    rows_ref[...] = in_ref[:, :, :width].reshape(slots, width)
    tail = in_ref[:, :, width:].reshape(slots, 128).astype(jnp.float32).T
    high, low = tail[0:1, :], tail[64:65, :]
    ids_ref[...] = jnp.where(high == 0.0, -1.0, (high - 1.0) * 128.0 + low).astype(jnp.int32)


def split_rows(arrived):
    devices, cap, wide = arrived.shape
    slots, width = devices * cap, wide - 128
    return pl.pallas_call(
        split_kernel,
        in_specs=vmem(1),
        out_specs=vmem(2),
        out_shape=[
            jax.ShapeDtypeStruct((slots, width), jnp.bfloat16),
            jax.ShapeDtypeStruct((1, slots), jnp.int32),
        ],
        compiler_params=params(),
        name="split",
        cost_estimate=pl.CostEstimate(flops=0, bytes_accessed=4 * slots * width, transcendentals=0),
    )(arrived)


def within_kernel(own0, own1, prior_ref, acc_ref):
    acc_ref[...] = jnp.full(acc_ref.shape, LOWEST, jnp.float32)
    acc_ref[OWN : OWN + 1, :] = prior_ref[...]
    own = [(0, 0), (1, 1)]
    update(acc_ref, OWN, own, own, lambda half: (own0, own1)[half])


def stage(name, own, arrays, heavy_pairs, light_pairs, where, found, after=()):
    names = list(arrays)
    size, width = arrays[names[0]].shape
    rows = found.shape[1]

    def run(*refs):
        held, refs = {"own0": refs[0], "own1": refs[1]}, refs[2:]
        inputs, where_ref, so_far_ref = refs[: len(names)], refs[len(names)], refs[len(names) + 1]
        acc_ref, buffers, sems = refs[-3:]
        acc_ref[...] = so_far_ref[...]
        compare(where_ref, 1, acc_ref, held, names, inputs, buffers, sems, heavy_pairs)
        if light_pairs:
            compare(where_ref, 0, acc_ref, held, names, inputs, buffers, sems, light_pairs)

    products = sum(len(a[1]) * len(b[1]) for a, b in heavy_pairs) / 4
    return pl.pallas_call(
        run,
        in_specs=vmem(2)
        + [pl.BlockSpec(memory_space=pl.ANY)] * len(names)
        + smem()
        + vmem(1)
        + vmem(len(after)),
        out_specs=pl.BlockSpec(memory_space=pltpu.VMEM),
        out_shape=jax.ShapeDtypeStruct(found.shape, jnp.float32),
        scratch_shapes=[pltpu.VMEM((len(names), size, width), jnp.bfloat16), pltpu.SemaphoreType.DMA((len(names),))],
        compiler_params=params(),
        name=name,
        cost_estimate=pl.CostEstimate(
            flops=int(2 * products * rows * rows * width),
            bytes_accessed=2 * len(names) * size * width,
            transcendentals=0,
        ),
    )(*own, *arrays.values(), where, found, *after)


def tie_kernel(array_ref, after_ref, out_ref):
    del array_ref, after_ref, out_ref


def tie(array, after):
    return pl.pallas_call(
        tie_kernel,
        in_specs=[pl.BlockSpec(memory_space=pl.ANY)] + vmem(1),
        out_specs=pl.BlockSpec(memory_space=pl.ANY),
        out_shape=jax.ShapeDtypeStruct(array.shape, array.dtype),
        input_output_aliases={0: 0},
        compiler_params=params(),
        name="tie",
        cost_estimate=pl.CostEstimate(flops=0, bytes_accessed=0, transcendentals=0),
    )(array, after)


def results_kernel(where_ref, so_far_ref, from_partner_ref, own_out, far_out, side_out):
    own_row = so_far_ref[OWN : OWN + 1, :]
    own_out[...] = jnp.where(where_ref[1] == 0, jnp.maximum(own_row, from_partner_ref[...]), own_row)
    near_partner_row = so_far_ref[NEAR_PARTNER : NEAR_PARTNER + 1, :]
    far_out[...] = jnp.where(where_ref[0] == 0, so_far_ref[FAR_PARTNER : FAR_PARTNER + 1, :], near_partner_row)
    side_out[...] = jnp.where(where_ref[1] == 1, so_far_ref[NEAR : NEAR + 1, :], near_partner_row)


def body(embeds, doc_ids, prior_max, owned, owned_ids, owner_dest):
    devices = lax.axis_size("grp") * lax.axis_size("blk")
    raw = embeds[0]
    rows, width = raw.shape
    core = lax.axis_index("grp") & 1
    heavy = (lax.axis_index("blk") + core) & 1
    where = jnp.stack([core, heavy]).astype(jnp.int32)

    def step(core):
        return 2 - 4 * core

    def to_heavy(core, heavy, block):
        return None if heavy else block ^ 1

    def to_light(core, heavy, block):
        return block ^ 1 if heavy else None

    def ahead(core, heavy, block):
        return block + step(core)

    def heavy_ahead(core, heavy, block):
        return block + step(core) if heavy else None

    def heavy_back(core, heavy, block):
        return block - step(core) if heavy else None

    outgoing = placed_rows(owned, owner_dest.reshape(1, -1), owned_ids.reshape(1, -1), devices)
    next_rows, next_ids = split_rows(lax.all_to_all(outgoing, BOTH, split_axis=0, concat_axis=0, tiled=True))

    line = jax.ShapeDtypeStruct((1, rows), jnp.float32)
    own0, own1 = (norm_half(raw, doc_ids, half) for half in range(2))
    partner0 = send(own0, to_heavy)
    near1 = send(own1, ahead)
    partner1 = send(own1, to_heavy)
    near0 = send(own0, heavy_ahead)

    found = pl.pallas_call(
        within_kernel,
        in_specs=vmem(3),
        out_specs=pl.BlockSpec(memory_space=pltpu.VMEM),
        out_shape=jax.ShapeDtypeStruct((8, rows), jnp.float32),
        compiler_params=params(),
        name="within",
        cost_estimate=pl.CostEstimate(
            flops=2 * rows * rows * width, bytes_accessed=2 * rows * width, transcendentals=0
        ),
    )(own0, own1, prior_max)
    far0 = send(partner0, heavy_back)
    near_partner0 = send(partner0, heavy_ahead)
    near_partner1 = send(near1, to_heavy)

    own = (OWN, [(0, "own0"), (1, "own1")])
    partner_both = (PARTNER, [(0, "partner0"), (1, "partner1")])
    near_both = (NEAR, [(0, "near0"), (1, "near1")])
    found = stage(
        "cross_a",
        (own0, own1),
        {"partner0": partner0, "near1": near1},
        [
            (own, (PARTNER, [(0, "partner0")])),
            (own, (NEAR, [(1, "near1")])),
            ((PARTNER, [(0, "partner0")]), (NEAR, [(1, "near1")])),
        ],
        [(own, (NEAR_PARTNER, [(1, "near1")]))],
        where,
        found,
    )
    partner1 = tie(partner1, found)
    far1 = send(partner1, heavy_back)
    found = stage(
        "cross_b",
        (own0, own1),
        {
            "partner1": partner1,
            "near0": near0,
            "near_partner0": near_partner0,
            "partner0": partner0,
            "near1": near1,
            "far0": far0,
        },
        [
            (own, (PARTNER, [(1, "partner1")])),
            (own, (NEAR, [(0, "near0")])),
            (own, (NEAR_PARTNER, [(0, "near_partner0")])),
            (partner_both, (NEAR_PARTNER, [(0, "near_partner0")])),
            (partner_both, (NEAR, [(0, "near0")])),
            ((PARTNER, [(1, "partner1")]), (NEAR, [(1, "near1")])),
            ((FAR_PARTNER, [(0, "far0")]), near_both),
        ],
        [],
        where,
        found,
        (next_ids,),
    )
    from_partner = send(found[PARTNER : PARTNER + 1], to_light)
    found = stage(
        "cross_c",
        (own0, own1),
        {"near_partner1": near_partner1, "far1": far1, "near0": near0, "near1": near1},
        [
            (own, (NEAR_PARTNER, [(1, "near_partner1")])),
            ((FAR_PARTNER, [(1, "far1")]), near_both),
        ],
        [],
        where,
        found,
        (),
    )
    mine, for_far, for_side = pl.pallas_call(
        results_kernel,
        in_specs=smem() + vmem(2),
        out_specs=vmem(3),
        out_shape=[line] * 3,
        compiler_params=params(),
        name="results",
    )(where, found, from_partner)
    from_far = send(for_far, lambda core, heavy, block: block + 1 + 2 * core if heavy else None)
    from_side = send(for_side, lambda core, heavy, block: block + 2 if core else None)
    lowest = jnp.float32(LOWEST)
    running = jnp.maximum(mine, jnp.where(heavy == 0, from_far, lowest))
    running = jnp.maximum(running, jnp.where(core == 1, from_side, lowest))
    return (running, next_rows, next_ids.reshape(-1))


def solution(mesh):
    return jax.shard_map(
        body,
        mesh=mesh,
        in_specs=(
            P("grp", "blk", None),
            P("grp", "blk"),
            P("grp", "blk"),
            P(("grp", "blk"), None),
            P(("grp", "blk")),
            P(("grp", "blk"), None),
        ),
        out_specs=(P("grp", "blk"), P(("grp", "blk"), None), P(("grp", "blk"))),
        check_vma=False,
    )
```

```python
import jax
import jax.numpy as jnp
from jax import lax
from jax.experimental import pallas as pl
from jax.experimental.pallas import tpu as pltpu
from jax.sharding import PartitionSpec as P

CAP = 4
LOWEST = -2.0
EXTRA = 16
AHEAD = 3
BOTH = ("grp", "blk")
OWN, PARTNER, NEAR, NEAR_PARTNER, FAR_PARTNER = range(5)


def normalize(matrix):
    values = matrix.astype(jnp.float32)
    scale = lax.rsqrt(jnp.sum(values * values, axis=-1, keepdims=True) + 1e-06)
    return (values * scale).astype(jnp.bfloat16)


def send(value, to):
    groups, members = lax.axis_size("grp"), lax.axis_size("blk")
    pairs = []
    for group in range(groups):
        for block in range(members):
            core = group % 2
            target = to(core, (block + core) % 2 == 1, block)
            if target is not None:
                pairs.append((group * members + block, group * members + target % members))
    return lax.ppermute(value, BOTH, pairs)


def params():
    return pltpu.CompilerParams(vmem_limit_bytes=24 * 1024 * 1024)


def vmem(n):
    return [pl.BlockSpec(memory_space=pltpu.VMEM)] * n


def smem():
    return [pl.BlockSpec(memory_space=pltpu.SMEM)]


def down(row):
    return jnp.broadcast_to(row, (128, row.shape[1])).T


def halves(numbers):
    numbers = numbers.astype(jnp.int32)
    return (numbers >> 7).astype(jnp.float32), (numbers & 127).astype(jnp.float32)


def numbers_of(ref):
    size = ref.shape[0] - EXTRA
    tail = ref[size:, :size].astype(jnp.float32)
    return (tail[0:1, :] * 128.0 + tail[1:2, :]).astype(jnp.int32)


def best(rows, row_ids, cols, col_down):
    scores = lax.dot_general(cols, rows, (((1,), (1,)), ((), ())), preferred_element_type=jnp.float32)
    found = []
    for left in range(0, rows.shape[0], 128):
        keep = col_down < row_ids[:, left : left + 128]
        part = jnp.where(keep, scores[:, left : left + 128], jnp.float32(LOWEST))
        found.append(jnp.max(part, axis=0, keepdims=True))
    return jnp.concatenate(found, axis=1)


def update(acc_ref, at_row, rows, cols, arrive):
    for _, col in cols:
        col_ref = arrive(col)
        size = col_ref.shape[0] - EXTRA
        col_down = down(numbers_of(col_ref))
        for half, row in rows:
            row_ref = arrive(row)
            row_ids = numbers_of(row_ref)
            for top in range(0, size, 256):
                found = best(row_ref[top : top + 256, :], row_ids[:, top : top + 256], col_ref[:size, :], col_down)
                at = slice(half * size + top, half * size + top + 256)
                acc_ref[at_row : at_row + 1, at] = jnp.maximum(acc_ref[at_row : at_row + 1, at], found)


def compare(where_ref, heavy, acc_ref, held, names, refs, buffers, sems, pairs):
    needed = [name for name in names if any(name == n for p in pairs for side in p for _, n in side[1])]

    def run(core):
        copies = {
            name: pltpu.make_async_copy(refs[names.index(name)], buffers.at[k], sems.at[k])
            for k, name in enumerate(needed)
        }
        started, there = set(), set()

        def arrive(name):
            if name in held:
                return held[name]
            if name not in there:
                for k, other in enumerate(needed):
                    if other not in started and k <= needed.index(name) + AHEAD:
                        copies[other].start()
                        started.add(other)
                copies[name].wait()
                there.add(name)
            return buffers.at[needed.index(name)]

        for (first, first_halves), (second, second_halves) in pairs:
            if core == 0:
                update(acc_ref, first, first_halves, second_halves, arrive)
            else:
                update(acc_ref, second, second_halves, first_halves, arrive)

    for core in (0, 1):

        @pl.when((where_ref[0] == core) & (where_ref[1] == heavy))
        def _():
            run(core)


def norm_kernel(x_ref, ids_ref, out_ref):
    size, width = x_ref.shape
    out_ref[:size, :] = normalize(x_ref[...])
    ids = jnp.concatenate([ids_ref[...], jnp.zeros((1, width - size), jnp.int32)], axis=1)
    high, low = halves(ids)
    row = lax.broadcasted_iota(jnp.int32, (EXTRA, width), 0)
    out_ref[size:, :] = jnp.where(row == 0, high, jnp.where(row == 1, low, 0.0)).astype(jnp.bfloat16)


def norm_half(embeds, ids, half):
    rows, width = embeds.shape
    size = rows // 2
    return pl.pallas_call(
        norm_kernel,
        grid=(1,),
        in_specs=[
            pl.BlockSpec((size, width), lambda i: (half, 0)),
            pl.BlockSpec((1, size), lambda i: (0, half)),
        ],
        out_specs=pl.BlockSpec((size + EXTRA, width), lambda i: (0, 0)),
        out_shape=jax.ShapeDtypeStruct((size + EXTRA, width), jnp.bfloat16),
        compiler_params=params(),
        name=f"norm_{half}",
        cost_estimate=pl.CostEstimate(flops=4 * size * width, bytes_accessed=4 * size * width, transcendentals=size),
    )(embeds, ids)


def place_kernel(rows_ref, target_ref, ids_ref, after_ref, out_ref):
    del after_ref
    count, width = rows_ref.shape
    target = target_ref[...]
    across = jnp.broadcast_to(target, (count, count))
    earlier = lax.broadcasted_iota(jnp.int32, (count, count), 0) < lax.broadcasted_iota(
        jnp.int32, (count, count), 1
    )
    same = (across.T == across) & earlier
    position = jnp.sum(same.astype(jnp.float32), axis=0, keepdims=True).astype(jnp.int32)
    place = target * CAP + position
    devices = out_ref.shape[0]
    slots = devices * CAP
    pick = (lax.broadcasted_iota(jnp.int32, (slots, count), 0) == place).astype(jnp.float32).astype(jnp.bfloat16)
    placed = jnp.dot(pick, normalize(rows_ref[...]), preferred_element_type=jnp.float32)
    out_ref[:, :, :width] = placed.astype(jnp.bfloat16).reshape(devices, CAP, width)
    high, low = halves(down(ids_ref[...]))
    lane = lax.broadcasted_iota(jnp.int32, high.shape, 1)
    pair = jnp.where(lane < 64, high + 1.0, low).astype(jnp.bfloat16)
    tail = jnp.dot(pick, pair, preferred_element_type=jnp.float32)
    out_ref[:, :, width:] = tail.astype(jnp.bfloat16).reshape(devices, CAP, 128)


def placed_rows(owned, target, ids, devices, after):
    count, width = owned.shape
    return pl.pallas_call(
        place_kernel,
        in_specs=vmem(4),
        out_specs=pl.BlockSpec(memory_space=pltpu.VMEM),
        out_shape=jax.ShapeDtypeStruct((devices, CAP, width + 128), jnp.bfloat16),
        compiler_params=params(),
        name="place",
        cost_estimate=pl.CostEstimate(
            flops=2 * devices * CAP * count * width, bytes_accessed=2 * (count + devices * CAP) * width, transcendentals=count
        ),
    )(owned, target, ids, after)


def split_kernel(in_ref, rows_ref, ids_ref):
    slots, width = rows_ref.shape
    rows_ref[...] = in_ref[:, :, :width].reshape(slots, width)
    tail = in_ref[:, :, width:].reshape(slots, 128).astype(jnp.float32).T
    high, low = tail[0:1, :], tail[64:65, :]
    ids_ref[...] = jnp.where(high == 0.0, -1.0, (high - 1.0) * 128.0 + low).astype(jnp.int32)


def split_rows(arrived):
    devices, cap, wide = arrived.shape
    slots, width = devices * cap, wide - 128
    return pl.pallas_call(
        split_kernel,
        in_specs=vmem(1),
        out_specs=vmem(2),
        out_shape=[
            jax.ShapeDtypeStruct((slots, width), jnp.bfloat16),
            jax.ShapeDtypeStruct((1, slots), jnp.int32),
        ],
        compiler_params=params(),
        name="split",
        cost_estimate=pl.CostEstimate(flops=0, bytes_accessed=4 * slots * width, transcendentals=0),
    )(arrived)


def within_kernel(own0, own1, prior_ref, acc_ref):
    acc_ref[...] = jnp.full(acc_ref.shape, LOWEST, jnp.float32)
    acc_ref[OWN : OWN + 1, :] = prior_ref[...]
    own = [(0, 0), (1, 1)]
    update(acc_ref, OWN, own, own, lambda half: (own0, own1)[half])


def stage(name, own, arrays, heavy_pairs, light_pairs, where, found, after=(), last=False):
    names = list(arrays)
    size, width = arrays[names[0]].shape
    rows = found.shape[1]

    def run(*refs):
        held, refs = {"own0": refs[0], "own1": refs[1]}, refs[2:]
        inputs, where_ref, so_far_ref = refs[: len(names)], refs[len(names)], refs[len(names) + 1]
        outs, (buffers, sems) = refs[len(names) + 2 + len(after) : -2], refs[-2:]
        acc_ref = outs[-1]
        acc_ref[...] = so_far_ref[...]
        compare(where_ref, 1, acc_ref, held, names, inputs, buffers, sems, heavy_pairs)
        if light_pairs:
            compare(where_ref, 0, acc_ref, held, names, inputs, buffers, sems, light_pairs)
        if last:
            own_out, far_out, side_out = outs[:3]
            own_row, from_partner = acc_ref[OWN : OWN + 1, :], refs[len(names) + 2][...]
            own_out[...] = jnp.where(where_ref[1] == 0, jnp.maximum(own_row, from_partner), own_row)
            near_partner_row = acc_ref[NEAR_PARTNER : NEAR_PARTNER + 1, :]
            far_out[...] = jnp.where(where_ref[0] == 0, acc_ref[FAR_PARTNER : FAR_PARTNER + 1, :], near_partner_row)
            side_out[...] = jnp.where(where_ref[1] == 1, acc_ref[NEAR : NEAR + 1, :], near_partner_row)

    products = sum(len(a[1]) * len(b[1]) for a, b in heavy_pairs) / 4
    return pl.pallas_call(
        run,
        in_specs=vmem(2)
        + [pl.BlockSpec(memory_space=pl.ANY)] * len(names)
        + smem()
        + vmem(1)
        + vmem(len(after)),
        out_specs=vmem(4 if last else 1),
        out_shape=[jax.ShapeDtypeStruct((1, rows), jnp.float32)] * (3 if last else 0)
        + [jax.ShapeDtypeStruct(found.shape, jnp.float32)],
        scratch_shapes=[pltpu.VMEM((len(names), size, width), jnp.bfloat16), pltpu.SemaphoreType.DMA((len(names),))],
        compiler_params=params(),
        name=name,
        cost_estimate=pl.CostEstimate(
            flops=int(2 * products * rows * rows * width),
            bytes_accessed=2 * len(names) * size * width,
            transcendentals=0,
        ),
    )(*own, *arrays.values(), where, found, *after)


def body(embeds, doc_ids, prior_max, owned, owned_ids, owner_dest):
    devices = lax.axis_size("grp") * lax.axis_size("blk")
    raw = embeds[0]
    rows, width = raw.shape
    core = lax.axis_index("grp") & 1
    heavy = (lax.axis_index("blk") + core) & 1
    where = jnp.stack([core, heavy]).astype(jnp.int32)

    def step(core):
        return 2 - 4 * core

    def to_heavy(core, heavy, block):
        return None if heavy else block ^ 1

    def to_light(core, heavy, block):
        return block ^ 1 if heavy else None

    def ahead(core, heavy, block):
        return block + step(core)

    def heavy_ahead(core, heavy, block):
        return block + step(core) if heavy else None

    def heavy_back(core, heavy, block):
        return block - step(core) if heavy else None

    own0, own1 = (norm_half(raw, doc_ids, half) for half in range(2))
    partner0 = send(own0, to_heavy)
    near1 = send(own1, ahead)
    partner1 = send(own1, to_heavy)
    near0 = send(own0, heavy_ahead)

    found = pl.pallas_call(
        within_kernel,
        in_specs=vmem(3),
        out_specs=pl.BlockSpec(memory_space=pltpu.VMEM),
        out_shape=jax.ShapeDtypeStruct((8, rows), jnp.float32),
        compiler_params=params(),
        name="within",
        cost_estimate=pl.CostEstimate(
            flops=2 * rows * rows * width, bytes_accessed=2 * rows * width, transcendentals=0
        ),
    )(own0, own1, prior_max)
    outgoing = placed_rows(owned, owner_dest.reshape(1, -1), owned_ids.reshape(1, -1), devices, found)
    next_rows, next_ids = split_rows(lax.all_to_all(outgoing, BOTH, split_axis=0, concat_axis=0, tiled=True))

    far0 = send(partner0, heavy_back)
    near_partner0 = send(partner0, heavy_ahead)
    near_partner1 = send(near1, to_heavy)

    own = (OWN, [(0, "own0"), (1, "own1")])
    partner_both = (PARTNER, [(0, "partner0"), (1, "partner1")])
    near_both = (NEAR, [(0, "near0"), (1, "near1")])
    (found,) = stage(
        "cross_a",
        (own0, own1),
        {"partner0": partner0, "near1": near1, "near0": near0},
        [
            (own, (PARTNER, [(0, "partner0")])),
            (own, (NEAR, [(1, "near1"), (0, "near0")])),
            ((PARTNER, [(0, "partner0")]), near_both),
        ],
        [(own, (NEAR_PARTNER, [(1, "near1")]))],
        where,
        found,
    )
    far1 = send(partner1, heavy_back)
    (found,) = stage(
        "cross_b",
        (own0, own1),
        {
            "partner1": partner1,
            "near1": near1,
            "near0": near0,
            "far0": far0,
            "near_partner0": near_partner0,
            "partner0": partner0,
        },
        [
            (own, (PARTNER, [(1, "partner1")])),
            ((PARTNER, [(1, "partner1")]), near_both),
            ((FAR_PARTNER, [(0, "far0")]), near_both),
            (own, (NEAR_PARTNER, [(0, "near_partner0")])),
            (partner_both, (NEAR_PARTNER, [(0, "near_partner0")])),
        ],
        [],
        where,
        found,
        (next_ids,),
    )
    from_partner = send(found[PARTNER : PARTNER + 1], to_light)
    mine, for_far, for_side, _ = stage(
        "cross_c",
        (own0, own1),
        {"near_partner1": near_partner1, "far1": far1, "near0": near0, "near1": near1},
        [
            (own, (NEAR_PARTNER, [(1, "near_partner1")])),
            ((FAR_PARTNER, [(1, "far1")]), near_both),
        ],
        [],
        where,
        found,
        (from_partner,),
        last=True,
    )
    from_far = send(for_far, lambda core, heavy, block: block + 1 + 2 * core if heavy else None)
    from_side = send(for_side, lambda core, heavy, block: block + 2 if core else None)
    lowest = jnp.float32(LOWEST)
    running = jnp.maximum(mine, jnp.where(heavy == 0, from_far, lowest))
    running = jnp.maximum(running, jnp.where(core == 1, from_side, lowest))
    return (running, next_rows, next_ids.reshape(-1))


def solution(mesh):
    return jax.shard_map(
        body,
        mesh=mesh,
        in_specs=(
            P("grp", "blk", None),
            P("grp", "blk"),
            P("grp", "blk"),
            P(("grp", "blk"), None),
            P(("grp", "blk")),
            P(("grp", "blk"), None),
        ),
        out_specs=(P("grp", "blk"), P(("grp", "blk"), None), P(("grp", "blk"))),
        check_vma=False,
    )
```

```python
import jax
import jax.numpy as jnp
from jax import lax
from jax.experimental import pallas as pl
from jax.experimental.pallas import tpu as pltpu
from jax.sharding import PartitionSpec as P

CAP = 4
LOWEST = -2.0
EXTRA = 16
AHEAD = 3
BOTH = ("grp", "blk")
OWN, PARTNER, NEAR, NEAR_PARTNER, FAR_PARTNER = range(5)


def normalize(matrix):
    values = matrix.astype(jnp.float32)
    scale = lax.rsqrt(jnp.sum(values * values, axis=-1, keepdims=True) + 1e-06)
    return (values * scale).astype(jnp.bfloat16)


def send(value, to):
    groups, members = lax.axis_size("grp"), lax.axis_size("blk")
    pairs = []
    for group in range(groups):
        for block in range(members):
            core = group % 2
            target = to(core, (block + core) % 2 == 1, block)
            if target is not None:
                pairs.append((group * members + block, group * members + target % members))
    return lax.ppermute(value, BOTH, pairs)


def params():
    return pltpu.CompilerParams(vmem_limit_bytes=24 * 1024 * 1024)


def vmem(n):
    return [pl.BlockSpec(memory_space=pltpu.VMEM)] * n


def smem():
    return [pl.BlockSpec(memory_space=pltpu.SMEM)]


def down(row):
    return jnp.broadcast_to(row, (128, row.shape[1])).T


def halves(numbers):
    numbers = numbers.astype(jnp.int32)
    return (numbers >> 7).astype(jnp.float32), (numbers & 127).astype(jnp.float32)


def numbers_of(ref):
    size = ref.shape[0] - EXTRA
    tail = ref[size:, :size].astype(jnp.float32)
    return (tail[0:1, :] * 128.0 + tail[1:2, :]).astype(jnp.int32)


def best(rows, row_ids, cols, col_down):
    scores = lax.dot_general(cols, rows, (((1,), (1,)), ((), ())), preferred_element_type=jnp.float32)
    found = []
    for left in range(0, rows.shape[0], 128):
        keep = col_down < row_ids[:, left : left + 128]
        part = jnp.where(keep, scores[:, left : left + 128], jnp.float32(LOWEST))
        found.append(jnp.max(part, axis=0, keepdims=True))
    return jnp.concatenate(found, axis=1)


def update(acc_ref, at_row, rows, cols, arrive):
    for _, col in cols:
        col_ref = arrive(col)
        size = col_ref.shape[0] - EXTRA
        col_down = down(numbers_of(col_ref))
        for half, row in rows:
            row_ref = arrive(row)
            row_ids = numbers_of(row_ref)
            for top in range(0, size, 256):
                found = best(row_ref[top : top + 256, :], row_ids[:, top : top + 256], col_ref[:size, :], col_down)
                at = slice(half * size + top, half * size + top + 256)
                acc_ref[at_row : at_row + 1, at] = jnp.maximum(acc_ref[at_row : at_row + 1, at], found)


def compare(where_ref, heavy, acc_ref, held, names, refs, buffers, sems, pairs):
    needed = [name for name in names if any(name == n for p in pairs for side in p for _, n in side[1])]

    def run(core):
        copies = {
            name: pltpu.make_async_copy(refs[names.index(name)], buffers.at[k], sems.at[k])
            for k, name in enumerate(needed)
        }
        started, there = set(), set()

        def arrive(name):
            if name in held:
                return held[name]
            if name not in there:
                for k, other in enumerate(needed):
                    if other not in started and k <= needed.index(name) + AHEAD:
                        copies[other].start()
                        started.add(other)
                copies[name].wait()
                there.add(name)
            return buffers.at[needed.index(name)]

        for (first, first_halves), (second, second_halves) in pairs:
            if core == 0:
                update(acc_ref, first, first_halves, second_halves, arrive)
            else:
                update(acc_ref, second, second_halves, first_halves, arrive)

    for core in (0, 1):

        @pl.when((where_ref[0] == core) & (where_ref[1] == heavy))
        def _():
            run(core)


def norm_kernel(x_ref, ids_ref, out_ref):
    size, width = x_ref.shape
    out_ref[:size, :] = normalize(x_ref[...])
    ids = jnp.concatenate([ids_ref[...], jnp.zeros((1, width - size), jnp.int32)], axis=1)
    high, low = halves(ids)
    row = lax.broadcasted_iota(jnp.int32, (EXTRA, width), 0)
    out_ref[size:, :] = jnp.where(row == 0, high, jnp.where(row == 1, low, 0.0)).astype(jnp.bfloat16)


def norm_half(embeds, ids, half):
    rows, width = embeds.shape
    size = rows // 2
    return pl.pallas_call(
        norm_kernel,
        grid=(1,),
        in_specs=[
            pl.BlockSpec((size, width), lambda i: (half, 0)),
            pl.BlockSpec((1, size), lambda i: (0, half)),
        ],
        out_specs=pl.BlockSpec((size + EXTRA, width), lambda i: (0, 0)),
        out_shape=jax.ShapeDtypeStruct((size + EXTRA, width), jnp.bfloat16),
        compiler_params=params(),
        name=f"norm_{half}",
        cost_estimate=pl.CostEstimate(flops=4 * size * width, bytes_accessed=4 * size * width, transcendentals=size),
    )(embeds, ids)


def place_kernel(rows_ref, target_ref, ids_ref, after_ref, out_ref):
    del after_ref
    count, width = rows_ref.shape
    target = target_ref[...]
    across = jnp.broadcast_to(target, (count, count))
    earlier = lax.broadcasted_iota(jnp.int32, (count, count), 0) < lax.broadcasted_iota(
        jnp.int32, (count, count), 1
    )
    same = (across.T == across) & earlier
    position = jnp.sum(same.astype(jnp.float32), axis=0, keepdims=True).astype(jnp.int32)
    place = target * CAP + position
    devices = out_ref.shape[0]
    slots = devices * CAP
    pick = (lax.broadcasted_iota(jnp.int32, (slots, count), 0) == place).astype(jnp.float32).astype(jnp.bfloat16)
    placed = jnp.dot(pick, normalize(rows_ref[...]), preferred_element_type=jnp.float32)
    out_ref[:, :, :width] = placed.astype(jnp.bfloat16).reshape(devices, CAP, width)
    high, low = halves(down(ids_ref[...]))
    lane = lax.broadcasted_iota(jnp.int32, high.shape, 1)
    pair = jnp.where(lane < 64, high + 1.0, low).astype(jnp.bfloat16)
    tail = jnp.dot(pick, pair, preferred_element_type=jnp.float32)
    out_ref[:, :, width:] = tail.astype(jnp.bfloat16).reshape(devices, CAP, 128)


def placed_rows(owned, target, ids, devices, after):
    count, width = owned.shape
    return pl.pallas_call(
        place_kernel,
        in_specs=vmem(4),
        out_specs=pl.BlockSpec(memory_space=pltpu.VMEM),
        out_shape=jax.ShapeDtypeStruct((devices, CAP, width + 128), jnp.bfloat16),
        compiler_params=params(),
        name="place",
        cost_estimate=pl.CostEstimate(
            flops=2 * devices * CAP * count * width, bytes_accessed=2 * (count + devices * CAP) * width, transcendentals=count
        ),
    )(owned, target, ids, after)


def split_kernel(in_ref, rows_ref, ids_ref):
    slots, width = rows_ref.shape
    rows_ref[...] = in_ref[:, :, :width].reshape(slots, width)
    tail = in_ref[:, :, width:].reshape(slots, 128).astype(jnp.float32).T
    high, low = tail[0:1, :], tail[64:65, :]
    ids_ref[...] = jnp.where(high == 0.0, -1.0, (high - 1.0) * 128.0 + low).astype(jnp.int32)


def split_rows(arrived):
    devices, cap, wide = arrived.shape
    slots, width = devices * cap, wide - 128
    return pl.pallas_call(
        split_kernel,
        in_specs=vmem(1),
        out_specs=vmem(2),
        out_shape=[
            jax.ShapeDtypeStruct((slots, width), jnp.bfloat16),
            jax.ShapeDtypeStruct((1, slots), jnp.int32),
        ],
        compiler_params=params(),
        name="split",
        cost_estimate=pl.CostEstimate(flops=0, bytes_accessed=4 * slots * width, transcendentals=0),
    )(arrived)


def within_kernel(own0, own1, prior_ref, acc_ref):
    acc_ref[...] = jnp.full(acc_ref.shape, LOWEST, jnp.float32)
    acc_ref[OWN : OWN + 1, :] = prior_ref[...]
    own = [(0, 0), (1, 1)]
    update(acc_ref, OWN, own, own, lambda half: (own0, own1)[half])


def stage(name, own, arrays, heavy_pairs, light_pairs, where, found, after=(), last=False):
    names = list(arrays)
    size, width = arrays[names[0]].shape
    rows = found.shape[1]

    def run(*refs):
        held, refs = {"own0": refs[0], "own1": refs[1]}, refs[2:]
        inputs, where_ref, so_far_ref = refs[: len(names)], refs[len(names)], refs[len(names) + 1]
        outs, (buffers, sems) = refs[len(names) + 2 + len(after) : -2], refs[-2:]
        acc_ref = outs[-1]
        acc_ref[...] = so_far_ref[...]
        compare(where_ref, 1, acc_ref, held, names, inputs, buffers, sems, heavy_pairs)
        if light_pairs:
            compare(where_ref, 0, acc_ref, held, names, inputs, buffers, sems, light_pairs)
        if last:
            own_out, partner_out, far_out, side_out = outs[:4]
            own_out[...] = acc_ref[OWN : OWN + 1, :]
            partner_out[...] = acc_ref[PARTNER : PARTNER + 1, :]
            near_partner_row = acc_ref[NEAR_PARTNER : NEAR_PARTNER + 1, :]
            far_out[...] = jnp.where(where_ref[0] == 0, acc_ref[FAR_PARTNER : FAR_PARTNER + 1, :], near_partner_row)
            side_out[...] = jnp.where(where_ref[1] == 1, acc_ref[NEAR : NEAR + 1, :], near_partner_row)

    products = sum(len(a[1]) * len(b[1]) for a, b in heavy_pairs) / 4
    return pl.pallas_call(
        run,
        in_specs=vmem(2)
        + [pl.BlockSpec(memory_space=pl.ANY)] * len(names)
        + smem()
        + vmem(1)
        + vmem(len(after)),
        out_specs=vmem(5 if last else 1),
        out_shape=[jax.ShapeDtypeStruct((1, rows), jnp.float32)] * (4 if last else 0)
        + [jax.ShapeDtypeStruct(found.shape, jnp.float32)],
        scratch_shapes=[pltpu.VMEM((len(names), size, width), jnp.bfloat16), pltpu.SemaphoreType.DMA((len(names),))],
        compiler_params=params(),
        name=name,
        cost_estimate=pl.CostEstimate(
            flops=int(2 * products * rows * rows * width),
            bytes_accessed=2 * len(names) * size * width,
            transcendentals=0,
        ),
    )(*own, *arrays.values(), where, found, *after)


def body(embeds, doc_ids, prior_max, owned, owned_ids, owner_dest):
    devices = lax.axis_size("grp") * lax.axis_size("blk")
    raw = embeds[0]
    rows, width = raw.shape
    core = lax.axis_index("grp") & 1
    heavy = (lax.axis_index("blk") + core) & 1
    where = jnp.stack([core, heavy]).astype(jnp.int32)

    def step(core):
        return 2 - 4 * core

    def to_heavy(core, heavy, block):
        return None if heavy else block ^ 1

    def to_light(core, heavy, block):
        return block ^ 1 if heavy else None

    def ahead(core, heavy, block):
        return block + step(core)

    def heavy_ahead(core, heavy, block):
        return block + step(core) if heavy else None

    def heavy_back(core, heavy, block):
        return block - step(core) if heavy else None

    own0, own1 = (norm_half(raw, doc_ids, half) for half in range(2))
    partner0 = send(own0, to_heavy)
    near1 = send(own1, ahead)
    partner1 = send(own1, to_heavy)
    near0 = send(own0, heavy_ahead)

    found = pl.pallas_call(
        within_kernel,
        in_specs=vmem(3),
        out_specs=pl.BlockSpec(memory_space=pltpu.VMEM),
        out_shape=jax.ShapeDtypeStruct((8, rows), jnp.float32),
        compiler_params=params(),
        name="within",
        cost_estimate=pl.CostEstimate(
            flops=2 * rows * rows * width, bytes_accessed=2 * rows * width, transcendentals=0
        ),
    )(own0, own1, prior_max)
    outgoing = placed_rows(owned, owner_dest.reshape(1, -1), owned_ids.reshape(1, -1), devices, found)
    next_rows, next_ids = split_rows(lax.all_to_all(outgoing, BOTH, split_axis=0, concat_axis=0, tiled=True))

    far0 = send(partner0, heavy_back)
    near_partner0 = send(partner0, heavy_ahead)
    near_partner1 = send(near1, to_heavy)
    far1 = send(partner1, heavy_back)

    own = (OWN, [(0, "own0"), (1, "own1")])
    partner_both = (PARTNER, [(0, "partner0"), (1, "partner1")])
    near_both = (NEAR, [(0, "near0"), (1, "near1")])
    (found,) = stage(
        "cross_a",
        (own0, own1),
        {"partner0": partner0, "near1": near1, "near0": near0, "partner1": partner1},
        [
            (own, (PARTNER, [(0, "partner0")])),
            (own, near_both),
            ((PARTNER, [(0, "partner0")]), near_both),
            (own, (PARTNER, [(1, "partner1")])),
            ((PARTNER, [(1, "partner1")]), near_both),
        ],
        [(own, (NEAR_PARTNER, [(1, "near1")]))],
        where,
        found,
    )
    mine, for_partner, for_far, for_side, _ = stage(
        "cross_b",
        (own0, own1),
        {
            "near_partner0": near_partner0,
            "near_partner1": near_partner1,
            "near0": near0,
            "far0": far0,
            "near1": near1,
            "far1": far1,
            "partner0": partner0,
            "partner1": partner1,
        },
        [
            (own, (NEAR_PARTNER, [(0, "near_partner0"), (1, "near_partner1")])),
            ((FAR_PARTNER, [(0, "far0")]), near_both),
            ((FAR_PARTNER, [(1, "far1")]), near_both),
            (partner_both, (NEAR_PARTNER, [(0, "near_partner0")])),
        ],
        [],
        where,
        found,
        (next_ids,),
        last=True,
    )
    from_partner = send(for_partner, to_light)
    from_far = send(for_far, lambda core, heavy, block: block + 1 + 2 * core if heavy else None)
    from_side = send(for_side, lambda core, heavy, block: block + 2 if core else None)
    lowest = jnp.float32(LOWEST)
    running = jnp.maximum(mine, jnp.where(heavy == 0, jnp.maximum(from_partner, from_far), lowest))
    running = jnp.maximum(running, jnp.where(core == 1, from_side, lowest))
    return (running, next_rows, next_ids.reshape(-1))


def solution(mesh):
    return jax.shard_map(
        body,
        mesh=mesh,
        in_specs=(
            P("grp", "blk", None),
            P("grp", "blk"),
            P("grp", "blk"),
            P(("grp", "blk"), None),
            P(("grp", "blk")),
            P(("grp", "blk"), None),
        ),
        out_specs=(P("grp", "blk"), P(("grp", "blk"), None), P(("grp", "blk"))),
        check_vma=False,
    )
```

```python
import jax
import jax.numpy as jnp
from jax import lax
from jax.experimental import pallas as pl
from jax.experimental.pallas import tpu as pltpu
from jax.sharding import PartitionSpec as P

CAP = 4
LOWEST = -2.0
EXTRA = 16
AHEAD = 3
BOTH = ("grp", "blk")
OWN, PARTNER, NEAR, NEAR_PARTNER, FAR_PARTNER = range(5)


def normalize(matrix):
    values = matrix.astype(jnp.float32)
    scale = lax.rsqrt(jnp.sum(values * values, axis=-1, keepdims=True) + 1e-06)
    return (values * scale).astype(jnp.bfloat16)


def send(value, to):
    groups, members = lax.axis_size("grp"), lax.axis_size("blk")
    pairs = []
    for group in range(groups):
        for block in range(members):
            core = group % 2
            target = to(core, (block + core) % 2 == 1, block)
            if target is not None:
                pairs.append((group * members + block, group * members + target % members))
    return lax.ppermute(value, BOTH, pairs)


def params():
    return pltpu.CompilerParams(vmem_limit_bytes=24 * 1024 * 1024)


def vmem(n):
    return [pl.BlockSpec(memory_space=pltpu.VMEM)] * n


def smem():
    return [pl.BlockSpec(memory_space=pltpu.SMEM)]


def down(row):
    return jnp.broadcast_to(row, (128, row.shape[1])).T


def halves(numbers):
    numbers = numbers.astype(jnp.int32)
    return (numbers >> 7).astype(jnp.float32), (numbers & 127).astype(jnp.float32)


def numbers_of(ref):
    size = ref.shape[0] - EXTRA
    tail = ref[size:, :size].astype(jnp.float32)
    return (tail[0:1, :] * 128.0 + tail[1:2, :]).astype(jnp.int32)


def best(rows, row_ids, cols, col_down):
    scores = lax.dot_general(cols, rows, (((1,), (1,)), ((), ())), preferred_element_type=jnp.float32)
    found = []
    for left in range(0, rows.shape[0], 128):
        keep = col_down < row_ids[:, left : left + 128]
        part = jnp.where(keep, scores[:, left : left + 128], jnp.float32(LOWEST))
        found.append(jnp.max(part, axis=0, keepdims=True))
    return jnp.concatenate(found, axis=1)


def update(acc_ref, at_row, rows, cols, arrive):
    for _, col in cols:
        col_ref = arrive(col)
        size = col_ref.shape[0] - EXTRA
        col_down = down(numbers_of(col_ref))
        for half, row in rows:
            row_ref = arrive(row)
            row_ids = numbers_of(row_ref)
            for top in range(0, size, 256):
                found = best(row_ref[top : top + 256, :], row_ids[:, top : top + 256], col_ref[:size, :], col_down)
                at = slice(half * size + top, half * size + top + 256)
                acc_ref[at_row : at_row + 1, at] = jnp.maximum(acc_ref[at_row : at_row + 1, at], found)


def compare(where_ref, heavy, acc_ref, held, names, refs, buffers, sems, pairs):
    needed = [name for name in names if any(name == n for p in pairs for side in p for _, n in side[1])]

    def run(core):
        copies = {
            name: pltpu.make_async_copy(refs[names.index(name)], buffers.at[k], sems.at[k])
            for k, name in enumerate(needed)
        }
        started, there = set(), set()

        def arrive(name):
            if name in held:
                return held[name]
            if name not in there:
                for k, other in enumerate(needed):
                    if other not in started and k <= needed.index(name) + AHEAD:
                        copies[other].start()
                        started.add(other)
                copies[name].wait()
                there.add(name)
            return buffers.at[needed.index(name)]

        for (first, first_halves), (second, second_halves) in pairs:
            if core == 0:
                update(acc_ref, first, first_halves, second_halves, arrive)
            else:
                update(acc_ref, second, second_halves, first_halves, arrive)

    for core in (0, 1):

        @pl.when((where_ref[0] == core) & (where_ref[1] == heavy))
        def _():
            run(core)


def norm_kernel(x_ref, ids_ref, out_ref):
    size, width = x_ref.shape
    out_ref[:size, :] = normalize(x_ref[...])
    ids = jnp.concatenate([ids_ref[...], jnp.zeros((1, width - size), jnp.int32)], axis=1)
    high, low = halves(ids)
    row = lax.broadcasted_iota(jnp.int32, (EXTRA, width), 0)
    out_ref[size:, :] = jnp.where(row == 0, high, jnp.where(row == 1, low, 0.0)).astype(jnp.bfloat16)


def norm_half(embeds, ids, half):
    rows, width = embeds.shape
    size = rows // 2
    return pl.pallas_call(
        norm_kernel,
        grid=(1,),
        in_specs=[
            pl.BlockSpec((size, width), lambda i: (half, 0)),
            pl.BlockSpec((1, size), lambda i: (0, half)),
        ],
        out_specs=pl.BlockSpec((size + EXTRA, width), lambda i: (0, 0)),
        out_shape=jax.ShapeDtypeStruct((size + EXTRA, width), jnp.bfloat16),
        compiler_params=params(),
        name=f"norm_{half}",
        cost_estimate=pl.CostEstimate(flops=4 * size * width, bytes_accessed=4 * size * width, transcendentals=size),
    )(embeds, ids)


def place_kernel(rows_ref, target_ref, ids_ref, after_ref, out_ref):
    del after_ref
    count, width = rows_ref.shape
    target = target_ref[...]
    across = jnp.broadcast_to(target, (count, count))
    earlier = lax.broadcasted_iota(jnp.int32, (count, count), 0) < lax.broadcasted_iota(
        jnp.int32, (count, count), 1
    )
    same = (across.T == across) & earlier
    position = jnp.sum(same.astype(jnp.float32), axis=0, keepdims=True).astype(jnp.int32)
    place = target * CAP + position
    devices = out_ref.shape[0]
    slots = devices * CAP
    pick = (lax.broadcasted_iota(jnp.int32, (slots, count), 0) == place).astype(jnp.float32).astype(jnp.bfloat16)
    placed = jnp.dot(pick, normalize(rows_ref[...]), preferred_element_type=jnp.float32)
    out_ref[:, :, :width] = placed.astype(jnp.bfloat16).reshape(devices, CAP, width)
    high, low = halves(down(ids_ref[...]))
    lane = lax.broadcasted_iota(jnp.int32, high.shape, 1)
    pair = jnp.where(lane < 64, high + 1.0, low).astype(jnp.bfloat16)
    tail = jnp.dot(pick, pair, preferred_element_type=jnp.float32)
    out_ref[:, :, width:] = tail.astype(jnp.bfloat16).reshape(devices, CAP, 128)


def placed_rows(owned, target, ids, devices, after):
    count, width = owned.shape
    return pl.pallas_call(
        place_kernel,
        in_specs=vmem(4),
        out_specs=pl.BlockSpec(memory_space=pltpu.VMEM),
        out_shape=jax.ShapeDtypeStruct((devices, CAP, width + 128), jnp.bfloat16),
        compiler_params=params(),
        name="place",
        cost_estimate=pl.CostEstimate(
            flops=2 * devices * CAP * count * width, bytes_accessed=2 * (count + devices * CAP) * width, transcendentals=count
        ),
    )(owned, target, ids, after)


def split_kernel(in_ref, rows_ref, ids_ref):
    slots, width = rows_ref.shape
    rows_ref[...] = in_ref[:, :, :width].reshape(slots, width)
    tail = in_ref[:, :, width:].reshape(slots, 128).astype(jnp.float32).T
    high, low = tail[0:1, :], tail[64:65, :]
    ids_ref[...] = jnp.where(high == 0.0, -1.0, (high - 1.0) * 128.0 + low).astype(jnp.int32)


def split_rows(arrived):
    devices, cap, wide = arrived.shape
    slots, width = devices * cap, wide - 128
    return pl.pallas_call(
        split_kernel,
        in_specs=vmem(1),
        out_specs=vmem(2),
        out_shape=[
            jax.ShapeDtypeStruct((slots, width), jnp.bfloat16),
            jax.ShapeDtypeStruct((1, slots), jnp.int32),
        ],
        compiler_params=params(),
        name="split",
        cost_estimate=pl.CostEstimate(flops=0, bytes_accessed=4 * slots * width, transcendentals=0),
    )(arrived)


def within_kernel(own0, own1, prior_ref, acc_ref):
    acc_ref[...] = jnp.full(acc_ref.shape, LOWEST, jnp.float32)
    acc_ref[OWN : OWN + 1, :] = prior_ref[...]
    own = [(0, 0), (1, 1)]
    update(acc_ref, OWN, own, own, lambda half: (own0, own1)[half])


def stage(name, own, arrays, heavy_pairs, light_pairs, where, found, after=(), last=False):
    names = list(arrays)
    size, width = arrays[names[0]].shape
    rows = found.shape[1]

    def run(*refs):
        held, refs = dict(zip(("own0", "own1"), refs[: len(own)])), refs[len(own) :]
        inputs, where_ref, so_far_ref = refs[: len(names)], refs[len(names)], refs[len(names) + 1]
        outs, (buffers, sems) = refs[len(names) + 2 + len(after) : -2], refs[-2:]
        acc_ref = outs[-1]
        acc_ref[...] = so_far_ref[...]
        compare(where_ref, 1, acc_ref, held, names, inputs, buffers, sems, heavy_pairs)
        if light_pairs:
            compare(where_ref, 0, acc_ref, held, names, inputs, buffers, sems, light_pairs)
        if last:
            own_out, far_out, side_out = outs[:3]
            own_row, from_partner = acc_ref[OWN : OWN + 1, :], refs[len(names) + 2][...]
            own_out[...] = jnp.where(where_ref[1] == 0, jnp.maximum(own_row, from_partner), own_row)
            near_partner_row = acc_ref[NEAR_PARTNER : NEAR_PARTNER + 1, :]
            far_out[...] = jnp.where(where_ref[0] == 0, acc_ref[FAR_PARTNER : FAR_PARTNER + 1, :], near_partner_row)
            side_out[...] = jnp.where(where_ref[1] == 1, acc_ref[NEAR : NEAR + 1, :], near_partner_row)

    products = sum(len(a[1]) * len(b[1]) for a, b in heavy_pairs) / 4
    return pl.pallas_call(
        run,
        in_specs=vmem(len(own))
        + [pl.BlockSpec(memory_space=pl.ANY)] * len(names)
        + smem()
        + vmem(1)
        + ([pl.BlockSpec(memory_space=pltpu.VMEM if last else pltpu.HBM)] * len(after)),
        out_specs=vmem(4 if last else 1),
        out_shape=[jax.ShapeDtypeStruct((1, rows), jnp.float32)] * (3 if last else 0)
        + [jax.ShapeDtypeStruct(found.shape, jnp.float32)],
        scratch_shapes=[pltpu.VMEM((len(names), size, width), jnp.bfloat16), pltpu.SemaphoreType.DMA((len(names),))],
        compiler_params=params(),
        name=name,
        cost_estimate=pl.CostEstimate(
            flops=int(2 * products * rows * rows * width),
            bytes_accessed=2 * len(names) * size * width,
            transcendentals=0,
        ),
    )(*own, *arrays.values(), where, found, *after)


def body(embeds, doc_ids, prior_max, owned, owned_ids, owner_dest):
    devices = lax.axis_size("grp") * lax.axis_size("blk")
    raw = embeds[0]
    rows, width = raw.shape
    core = lax.axis_index("grp") & 1
    heavy = (lax.axis_index("blk") + core) & 1
    where = jnp.stack([core, heavy]).astype(jnp.int32)

    def step(core):
        return 2 - 4 * core

    def to_heavy(core, heavy, block):
        return None if heavy else block ^ 1

    def to_light(core, heavy, block):
        return block ^ 1 if heavy else None

    def ahead(core, heavy, block):
        return block + step(core)

    def heavy_ahead(core, heavy, block):
        return block + step(core) if heavy else None

    def heavy_back(core, heavy, block):
        return block - step(core) if heavy else None

    own0, own1 = (norm_half(raw, doc_ids, half) for half in range(2))
    partner0 = send(own0, to_heavy)
    near1 = send(own1, ahead)
    partner1 = send(own1, to_heavy)
    near0 = send(own0, heavy_ahead)

    found = pl.pallas_call(
        within_kernel,
        in_specs=vmem(3),
        out_specs=pl.BlockSpec(memory_space=pltpu.VMEM),
        out_shape=jax.ShapeDtypeStruct((8, rows), jnp.float32),
        compiler_params=params(),
        name="within",
        cost_estimate=pl.CostEstimate(
            flops=2 * rows * rows * width, bytes_accessed=2 * rows * width, transcendentals=0
        ),
    )(own0, own1, prior_max)
    outgoing = placed_rows(owned, owner_dest.reshape(1, -1), owned_ids.reshape(1, -1), devices, found)
    next_rows, next_ids = split_rows(lax.all_to_all(outgoing, BOTH, split_axis=0, concat_axis=0, tiled=True))

    far0 = send(partner0, heavy_back)
    near_partner0 = send(partner0, heavy_ahead)
    near_partner1 = send(near1, to_heavy)
    far1 = send(partner1, heavy_back)

    own = (OWN, [(0, "own0"), (1, "own1")])
    partner_both = (PARTNER, [(0, "partner0"), (1, "partner1")])
    near_both = (NEAR, [(0, "near0"), (1, "near1")])
    (found,) = stage(
        "cross_a",
        (own0, own1),
        {"partner0": partner0, "near1": near1, "near0": near0, "partner1": partner1},
        [
            (own, (PARTNER, [(0, "partner0")])),
            (own, near_both),
            ((PARTNER, [(0, "partner0")]), near_both),
            (own, (PARTNER, [(1, "partner1")])),
            ((PARTNER, [(1, "partner1")]), near_both),
        ],
        [(own, (NEAR_PARTNER, [(1, "near1")]))],
        where,
        found,
    )
    (found,) = stage(
        "cross_b",
        (own0, own1),
        {
            "near0": near0,
            "far0": far0,
            "near1": near1,
            "near_partner0": near_partner0,
            "near_partner1": near_partner1,
            "partner0": partner0,
            "partner1": partner1,
        },
        [
            ((FAR_PARTNER, [(0, "far0")]), near_both),
            (own, (NEAR_PARTNER, [(0, "near_partner0"), (1, "near_partner1")])),
            (partner_both, (NEAR_PARTNER, [(0, "near_partner0")])),
        ],
        [],
        where,
        found,
        (next_ids,),
    )
    from_partner = send(found[PARTNER : PARTNER + 1], to_light)
    mine, for_far, for_side, _ = stage(
        "cross_c",
        (),
        {"far1": far1, "near0": near0, "near1": near1},
        [((FAR_PARTNER, [(1, "far1")]), near_both)],
        [],
        where,
        found,
        (from_partner,),
        last=True,
    )
    from_far = send(for_far, lambda core, heavy, block: block + 1 + 2 * core if heavy else None)
    from_side = send(for_side, lambda core, heavy, block: block + 2 if core else None)
    lowest = jnp.float32(LOWEST)
    running = jnp.maximum(mine, jnp.where(heavy == 0, from_far, lowest))
    running = jnp.maximum(running, jnp.where(core == 1, from_side, lowest))
    return (running, next_rows, next_ids.reshape(-1))


def solution(mesh):
    return jax.shard_map(
        body,
        mesh=mesh,
        in_specs=(
            P("grp", "blk", None),
            P("grp", "blk"),
            P("grp", "blk"),
            P(("grp", "blk"), None),
            P(("grp", "blk")),
            P(("grp", "blk"), None),
        ),
        out_specs=(P("grp", "blk"), P(("grp", "blk"), None), P(("grp", "blk"))),
        check_vma=False,
    )
```

```python
import jax
import jax.numpy as jnp
from jax import lax
from jax.experimental import pallas as pl
from jax.experimental.pallas import tpu as pltpu
from jax.sharding import PartitionSpec as P

CAP = 4
LOWEST = -2.0
EXTRA = 16
BOTH = ("grp", "blk")
OWN, PARTNER, NEAR, NEAR_PARTNER, FAR_PARTNER = range(5)


def normalize(matrix):
    values = matrix.astype(jnp.float32)
    scale = lax.rsqrt(jnp.sum(values * values, axis=-1, keepdims=True) + 1e-06)
    return (values * scale).astype(jnp.bfloat16)


def send(value, to):
    groups, members = lax.axis_size("grp"), lax.axis_size("blk")
    pairs = []
    for group in range(groups):
        for block in range(members):
            core = group % 2
            target = to(core, (block + core) % 2 == 1, block)
            if target is not None:
                pairs.append((group * members + block, group * members + target % members))
    return lax.ppermute(value, BOTH, pairs)


def params():
    return pltpu.CompilerParams(vmem_limit_bytes=24 * 1024 * 1024)


def vmem(n):
    return [pl.BlockSpec(memory_space=pltpu.VMEM)] * n


def smem():
    return [pl.BlockSpec(memory_space=pltpu.SMEM)]


def down(row):
    return jnp.broadcast_to(row, (128, row.shape[1])).T


def halves(numbers):
    numbers = numbers.astype(jnp.int32)
    return (numbers >> 7).astype(jnp.float32), (numbers & 127).astype(jnp.float32)


def numbers_of(ref):
    size = ref.shape[0] - EXTRA
    tail = ref[size:, :size].astype(jnp.float32)
    return (tail[0:1, :] * 128.0 + tail[1:2, :]).astype(jnp.int32)


def best(rows, row_ids, cols, col_down):
    scores = lax.dot_general(cols, rows, (((1,), (1,)), ((), ())), preferred_element_type=jnp.float32)
    found = []
    for left in range(0, rows.shape[0], 128):
        keep = col_down < row_ids[:, left : left + 128]
        part = jnp.where(keep, scores[:, left : left + 128], jnp.float32(LOWEST))
        found.append(jnp.max(part, axis=0, keepdims=True))
    return jnp.concatenate(found, axis=1)


def update(acc_ref, at_row, rows, cols, arrive):
    for _, col in cols:
        col_ref = arrive(col)
        size = col_ref.shape[0] - EXTRA
        col_down = down(numbers_of(col_ref))
        for half, row in rows:
            row_ref = arrive(row)
            row_ids = numbers_of(row_ref)
            for top in range(0, size, 256):
                found = best(row_ref[top : top + 256, :], row_ids[:, top : top + 256], col_ref[:size, :], col_down)
                at = slice(half * size + top, half * size + top + 256)
                acc_ref[at_row : at_row + 1, at] = jnp.maximum(acc_ref[at_row : at_row + 1, at], found)


def compare(where_ref, heavy, acc_ref, held, names, refs, buffers, sems, pairs):
    needed = [name for name in names if any(name == n for p in pairs for side in p for _, n in side[1])]

    def run(core):
        copies = {
            name: pltpu.make_async_copy(refs[names.index(name)], buffers.at[k], sems.at[k])
            for k, name in enumerate(needed)
        }
        for copy in copies.values():
            copy.start()
        for copy in copies.values():
            copy.wait()

        def arrive(name):
            return held[name] if name in held else buffers.at[needed.index(name)]

        for (first, first_halves), (second, second_halves) in pairs:
            if core == 0:
                update(acc_ref, first, first_halves, second_halves, arrive)
            else:
                update(acc_ref, second, second_halves, first_halves, arrive)

    for core in (0, 1):

        @pl.when((where_ref[0] == core) & (where_ref[1] == heavy))
        def _():
            run(core)


def norm_kernel(x_ref, ids_ref, out_ref):
    size, width = x_ref.shape
    out_ref[:size, :] = normalize(x_ref[...])
    ids = jnp.concatenate([ids_ref[...], jnp.zeros((1, width - size), jnp.int32)], axis=1)
    high, low = halves(ids)
    row = lax.broadcasted_iota(jnp.int32, (EXTRA, width), 0)
    out_ref[size:, :] = jnp.where(row == 0, high, jnp.where(row == 1, low, 0.0)).astype(jnp.bfloat16)


def norm_half(embeds, ids, half):
    rows, width = embeds.shape
    size = rows // 2
    return pl.pallas_call(
        norm_kernel,
        grid=(1,),
        in_specs=[
            pl.BlockSpec((size, width), lambda i: (half, 0)),
            pl.BlockSpec((1, size), lambda i: (0, half)),
        ],
        out_specs=pl.BlockSpec((size + EXTRA, width), lambda i: (0, 0)),
        out_shape=jax.ShapeDtypeStruct((size + EXTRA, width), jnp.bfloat16),
        compiler_params=params(),
        name=f"norm_{half}",
        cost_estimate=pl.CostEstimate(flops=4 * size * width, bytes_accessed=4 * size * width, transcendentals=size),
    )(embeds, ids)


def place_kernel(rows_ref, target_ref, ids_ref, after_ref, out_ref):
    del after_ref
    count, width = rows_ref.shape
    target = target_ref[...]
    across = jnp.broadcast_to(target, (count, count))
    earlier = lax.broadcasted_iota(jnp.int32, (count, count), 0) < lax.broadcasted_iota(
        jnp.int32, (count, count), 1
    )
    same = (across.T == across) & earlier
    position = jnp.sum(same.astype(jnp.float32), axis=0, keepdims=True).astype(jnp.int32)
    place = target * CAP + position
    devices = out_ref.shape[0]
    slots = devices * CAP
    pick = (lax.broadcasted_iota(jnp.int32, (slots, count), 0) == place).astype(jnp.float32).astype(jnp.bfloat16)
    placed = jnp.dot(pick, normalize(rows_ref[...]), preferred_element_type=jnp.float32)
    out_ref[:, :, :width] = placed.astype(jnp.bfloat16).reshape(devices, CAP, width)
    high, low = halves(down(ids_ref[...]))
    lane = lax.broadcasted_iota(jnp.int32, high.shape, 1)
    pair = jnp.where(lane < 64, high + 1.0, low).astype(jnp.bfloat16)
    tail = jnp.dot(pick, pair, preferred_element_type=jnp.float32)
    out_ref[:, :, width:] = tail.astype(jnp.bfloat16).reshape(devices, CAP, 128)


def placed_rows(owned, target, ids, devices, after):
    count, width = owned.shape
    return pl.pallas_call(
        place_kernel,
        in_specs=vmem(4),
        out_specs=pl.BlockSpec(memory_space=pltpu.VMEM),
        out_shape=jax.ShapeDtypeStruct((devices, CAP, width + 128), jnp.bfloat16),
        compiler_params=params(),
        name="place",
        cost_estimate=pl.CostEstimate(
            flops=2 * devices * CAP * count * width, bytes_accessed=2 * (count + devices * CAP) * width, transcendentals=count
        ),
    )(owned, target, ids, after)


def split_kernel(in_ref, rows_ref, ids_ref):
    slots, width = rows_ref.shape
    rows_ref[...] = in_ref[:, :, :width].reshape(slots, width)
    tail = in_ref[:, :, width:].reshape(slots, 128).astype(jnp.float32).T
    high, low = tail[0:1, :], tail[64:65, :]
    ids_ref[...] = jnp.where(high == 0.0, -1.0, (high - 1.0) * 128.0 + low).astype(jnp.int32)


def split_rows(arrived):
    devices, cap, wide = arrived.shape
    slots, width = devices * cap, wide - 128
    return pl.pallas_call(
        split_kernel,
        in_specs=vmem(1),
        out_specs=vmem(2),
        out_shape=[
            jax.ShapeDtypeStruct((slots, width), jnp.bfloat16),
            jax.ShapeDtypeStruct((1, slots), jnp.int32),
        ],
        compiler_params=params(),
        name="split",
        cost_estimate=pl.CostEstimate(flops=0, bytes_accessed=4 * slots * width, transcendentals=0),
    )(arrived)


def within_kernel(own0, own1, prior_ref, acc_ref):
    acc_ref[...] = jnp.full(acc_ref.shape, LOWEST, jnp.float32)
    acc_ref[OWN : OWN + 1, :] = prior_ref[...]
    own = [(0, 0), (1, 1)]
    update(acc_ref, OWN, own, own, lambda half: (own0, own1)[half])


def stage(name, own, arrays, heavy_pairs, light_pairs, where, found, after=(), last=False):
    names = list(arrays)
    size, width = arrays[names[0]].shape
    rows = found.shape[1]

    def run(*refs):
        held, refs = dict(zip(("own0", "own1"), refs[: len(own)])), refs[len(own) :]
        inputs, where_ref, so_far_ref = refs[: len(names)], refs[len(names)], refs[len(names) + 1]
        outs, (buffers, sems) = refs[len(names) + 2 + len(after) : -2], refs[-2:]
        acc_ref = outs[-1]
        acc_ref[...] = so_far_ref[...]
        compare(where_ref, 1, acc_ref, held, names, inputs, buffers, sems, heavy_pairs)
        if light_pairs:
            compare(where_ref, 0, acc_ref, held, names, inputs, buffers, sems, light_pairs)
        if last:
            own_out, far_out, side_out = outs[:3]
            own_row, from_partner = acc_ref[OWN : OWN + 1, :], refs[len(names) + 2][...]
            own_out[...] = jnp.where(where_ref[1] == 0, jnp.maximum(own_row, from_partner), own_row)
            near_partner_row = acc_ref[NEAR_PARTNER : NEAR_PARTNER + 1, :]
            far_out[...] = jnp.where(where_ref[0] == 0, acc_ref[FAR_PARTNER : FAR_PARTNER + 1, :], near_partner_row)
            side_out[...] = jnp.where(where_ref[1] == 1, acc_ref[NEAR : NEAR + 1, :], near_partner_row)

    products = sum(len(a[1]) * len(b[1]) for a, b in heavy_pairs) / 4
    return pl.pallas_call(
        run,
        in_specs=vmem(len(own))
        + [pl.BlockSpec(memory_space=pl.ANY)] * len(names)
        + smem()
        + vmem(1)
        + ([pl.BlockSpec(memory_space=pltpu.VMEM if last else pltpu.HBM)] * len(after)),
        out_specs=vmem(4 if last else 1),
        out_shape=[jax.ShapeDtypeStruct((1, rows), jnp.float32)] * (3 if last else 0)
        + [jax.ShapeDtypeStruct(found.shape, jnp.float32)],
        scratch_shapes=[pltpu.VMEM((len(names), size, width), jnp.bfloat16), pltpu.SemaphoreType.DMA((len(names),))],
        compiler_params=params(),
        name=name,
        cost_estimate=pl.CostEstimate(
            flops=int(2 * products * rows * rows * width),
            bytes_accessed=2 * len(names) * size * width,
            transcendentals=0,
        ),
    )(*own, *arrays.values(), where, found, *after)


def body(embeds, doc_ids, prior_max, owned, owned_ids, owner_dest):
    devices = lax.axis_size("grp") * lax.axis_size("blk")
    raw = embeds[0]
    rows, width = raw.shape
    core = lax.axis_index("grp") & 1
    heavy = (lax.axis_index("blk") + core) & 1
    where = jnp.stack([core, heavy]).astype(jnp.int32)

    def step(core):
        return 2 - 4 * core

    def to_heavy(core, heavy, block):
        return None if heavy else block ^ 1

    def to_light(core, heavy, block):
        return block ^ 1 if heavy else None

    def ahead(core, heavy, block):
        return block + step(core)

    def heavy_ahead(core, heavy, block):
        return block + step(core) if heavy else None

    def heavy_back(core, heavy, block):
        return block - step(core) if heavy else None

    own0, own1 = (norm_half(raw, doc_ids, half) for half in range(2))
    partner0 = send(own0, to_heavy)
    near1 = send(own1, ahead)
    partner1 = send(own1, to_heavy)
    near0 = send(own0, heavy_ahead)

    found = pl.pallas_call(
        within_kernel,
        in_specs=vmem(3),
        out_specs=pl.BlockSpec(memory_space=pltpu.VMEM),
        out_shape=jax.ShapeDtypeStruct((8, rows), jnp.float32),
        compiler_params=params(),
        name="within",
        cost_estimate=pl.CostEstimate(
            flops=2 * rows * rows * width, bytes_accessed=2 * rows * width, transcendentals=0
        ),
    )(own0, own1, prior_max)
    outgoing = placed_rows(owned, owner_dest.reshape(1, -1), owned_ids.reshape(1, -1), devices, found)
    next_rows, next_ids = split_rows(lax.all_to_all(outgoing, BOTH, split_axis=0, concat_axis=0, tiled=True))

    far0 = send(partner0, heavy_back)
    near_partner0 = send(partner0, heavy_ahead)
    near_partner1 = send(near1, to_heavy)
    far1 = send(partner1, heavy_back)

    own = (OWN, [(0, "own0"), (1, "own1")])
    partner_both = (PARTNER, [(0, "partner0"), (1, "partner1")])
    near_both = (NEAR, [(0, "near0"), (1, "near1")])
    (found,) = stage(
        "cross_a",
        (own0, own1),
        {"partner0": partner0, "near1": near1, "near0": near0, "partner1": partner1},
        [
            (own, (PARTNER, [(0, "partner0")])),
            (own, near_both),
            ((PARTNER, [(0, "partner0")]), near_both),
            (own, (PARTNER, [(1, "partner1")])),
            ((PARTNER, [(1, "partner1")]), near_both),
        ],
        [(own, (NEAR_PARTNER, [(1, "near1")]))],
        where,
        found,
    )
    (found,) = stage(
        "cross_b",
        (own0, own1),
        {
            "near0": near0,
            "far0": far0,
            "near1": near1,
            "near_partner0": near_partner0,
            "near_partner1": near_partner1,
            "partner0": partner0,
            "partner1": partner1,
        },
        [
            ((FAR_PARTNER, [(0, "far0")]), near_both),
            (own, (NEAR_PARTNER, [(0, "near_partner0"), (1, "near_partner1")])),
            (partner_both, (NEAR_PARTNER, [(0, "near_partner0")])),
        ],
        [],
        where,
        found,
        (next_ids,),
    )
    from_partner = send(found[PARTNER : PARTNER + 1], to_light)
    mine, for_far, for_side, _ = stage(
        "cross_c",
        (),
        {"far1": far1, "near0": near0, "near1": near1},
        [((FAR_PARTNER, [(1, "far1")]), near_both)],
        [],
        where,
        found,
        (from_partner,),
        last=True,
    )
    from_far = send(for_far, lambda core, heavy, block: block + 1 + 2 * core if heavy else None)
    from_side = send(for_side, lambda core, heavy, block: block + 2 if core else None)
    lowest = jnp.float32(LOWEST)
    running = jnp.maximum(mine, jnp.where(heavy == 0, from_far, lowest))
    running = jnp.maximum(running, jnp.where(core == 1, from_side, lowest))
    return (running, next_rows, next_ids.reshape(-1))


def solution(mesh):
    return jax.shard_map(
        body,
        mesh=mesh,
        in_specs=(
            P("grp", "blk", None),
            P("grp", "blk"),
            P("grp", "blk"),
            P(("grp", "blk"), None),
            P(("grp", "blk")),
            P(("grp", "blk"), None),
        ),
        out_specs=(P("grp", "blk"), P(("grp", "blk"), None), P(("grp", "blk"))),
        check_vma=False,
    )
```

```python
import jax
import jax.numpy as jnp
from jax import lax
from jax.experimental import pallas as pl
from jax.experimental.pallas import tpu as pltpu
from jax.sharding import PartitionSpec as P

CAP = 4
LOWEST = -2.0
EXTRA = 16
AHEAD = 3
BOTH = ("grp", "blk")
OWN, PARTNER, NEAR, NEAR_PARTNER, FAR_PARTNER = range(5)


def normalize(matrix):
    values = matrix.astype(jnp.float32)
    scale = lax.rsqrt(jnp.sum(values * values, axis=-1, keepdims=True) + 1e-06)
    return (values * scale).astype(jnp.bfloat16)


def send(value, to):
    groups, members = lax.axis_size("grp"), lax.axis_size("blk")
    pairs = []
    for group in range(groups):
        for block in range(members):
            core = group % 2
            target = to(core, (block + core) % 2 == 1, block)
            if target is not None:
                pairs.append((group * members + block, group * members + target % members))
    return lax.ppermute(value, BOTH, pairs)


def params():
    return pltpu.CompilerParams(vmem_limit_bytes=24 * 1024 * 1024)


def vmem(n):
    return [pl.BlockSpec(memory_space=pltpu.VMEM)] * n


def smem():
    return [pl.BlockSpec(memory_space=pltpu.SMEM)]


def down(row):
    return jnp.broadcast_to(row, (128, row.shape[1])).T


def halves(numbers):
    numbers = numbers.astype(jnp.int32)
    return (numbers >> 7).astype(jnp.float32), (numbers & 127).astype(jnp.float32)


def numbers_of(ref):
    size = ref.shape[0] - EXTRA
    tail = ref[size:, :size].astype(jnp.float32)
    return (tail[0:1, :] * 128.0 + tail[1:2, :]).astype(jnp.int32)


def best(rows, row_ids, cols, col_down):
    scores = lax.dot_general(cols, rows, (((1,), (1,)), ((), ())), preferred_element_type=jnp.float32)
    found = []
    for left in range(0, rows.shape[0], 128):
        keep = col_down < row_ids[:, left : left + 128]
        part = jnp.where(keep, scores[:, left : left + 128], jnp.float32(LOWEST))
        found.append(jnp.max(part, axis=0, keepdims=True))
    return jnp.concatenate(found, axis=1)


def update(acc_ref, at_row, rows, cols, arrive):
    for _, col in cols:
        col_ref = arrive(col)
        size = col_ref.shape[0] - EXTRA
        col_down = down(numbers_of(col_ref))
        for half, row in rows:
            row_ref = arrive(row)
            row_ids = numbers_of(row_ref)
            for top in range(0, size, 256):
                found = best(row_ref[top : top + 256, :], row_ids[:, top : top + 256], col_ref[:size, :], col_down)
                at = slice(half * size + top, half * size + top + 256)
                acc_ref[at_row : at_row + 1, at] = jnp.maximum(acc_ref[at_row : at_row + 1, at], found)


def compare(where_ref, heavy, acc_ref, held, names, refs, buffers, sems, pairs):
    needed = [name for name in names if any(name == n for p in pairs for side in p for _, n in side[1])]

    def run(core):
        copies = {
            name: pltpu.make_async_copy(refs[names.index(name)], buffers.at[k], sems.at[k])
            for k, name in enumerate(needed)
        }
        started, there = set(), set()

        def arrive(name):
            if name in held:
                return held[name]
            if name not in there:
                for k, other in enumerate(needed):
                    if other not in started and k <= needed.index(name) + AHEAD:
                        copies[other].start()
                        started.add(other)
                copies[name].wait()
                there.add(name)
            return buffers.at[needed.index(name)]

        for (first, first_halves), (second, second_halves) in pairs:
            if core == 0:
                update(acc_ref, first, first_halves, second_halves, arrive)
            else:
                update(acc_ref, second, second_halves, first_halves, arrive)

    for core in (0, 1):

        @pl.when((where_ref[0] == core) & (where_ref[1] == heavy))
        def _():
            run(core)


def norm_kernel(x_ref, ids_ref, out_ref):
    size, width = x_ref.shape
    out_ref[:size, :] = normalize(x_ref[...])
    ids = jnp.concatenate([ids_ref[...], jnp.zeros((1, width - size), jnp.int32)], axis=1)
    high, low = halves(ids)
    row = lax.broadcasted_iota(jnp.int32, (EXTRA, width), 0)
    out_ref[size:, :] = jnp.where(row == 0, high, jnp.where(row == 1, low, 0.0)).astype(jnp.bfloat16)


def norm_half(embeds, ids, half):
    rows, width = embeds.shape
    size = rows // 2
    return pl.pallas_call(
        norm_kernel,
        grid=(1,),
        in_specs=[
            pl.BlockSpec((size, width), lambda i: (half, 0)),
            pl.BlockSpec((1, size), lambda i: (0, half)),
        ],
        out_specs=pl.BlockSpec((size + EXTRA, width), lambda i: (0, 0)),
        out_shape=jax.ShapeDtypeStruct((size + EXTRA, width), jnp.bfloat16),
        compiler_params=params(),
        name=f"norm_{half}",
        cost_estimate=pl.CostEstimate(flops=4 * size * width, bytes_accessed=4 * size * width, transcendentals=size),
    )(embeds, ids)


def place_kernel(rows_ref, target_ref, ids_ref, after_ref, out_ref):
    del after_ref
    count, width = rows_ref.shape
    target = target_ref[...]
    across = jnp.broadcast_to(target, (count, count))
    earlier = lax.broadcasted_iota(jnp.int32, (count, count), 0) < lax.broadcasted_iota(
        jnp.int32, (count, count), 1
    )
    same = (across.T == across) & earlier
    position = jnp.sum(same.astype(jnp.float32), axis=0, keepdims=True).astype(jnp.int32)
    place = target * CAP + position
    devices = out_ref.shape[0]
    slots = devices * CAP
    pick = (lax.broadcasted_iota(jnp.int32, (slots, count), 0) == place).astype(jnp.float32).astype(jnp.bfloat16)
    placed = jnp.dot(pick, normalize(rows_ref[...]), preferred_element_type=jnp.float32)
    out_ref[:, :, :width] = placed.astype(jnp.bfloat16).reshape(devices, CAP, width)
    high, low = halves(down(ids_ref[...]))
    lane = lax.broadcasted_iota(jnp.int32, high.shape, 1)
    pair = jnp.where(lane < 64, high + 1.0, low).astype(jnp.bfloat16)
    tail = jnp.dot(pick, pair, preferred_element_type=jnp.float32)
    out_ref[:, :, width:] = tail.astype(jnp.bfloat16).reshape(devices, CAP, 128)


def placed_rows(owned, target, ids, devices, after):
    count, width = owned.shape
    return pl.pallas_call(
        place_kernel,
        in_specs=vmem(4),
        out_specs=pl.BlockSpec(memory_space=pltpu.VMEM),
        out_shape=jax.ShapeDtypeStruct((devices, CAP, width + 128), jnp.bfloat16),
        compiler_params=params(),
        name="place",
        cost_estimate=pl.CostEstimate(
            flops=2 * devices * CAP * count * width, bytes_accessed=2 * (count + devices * CAP) * width, transcendentals=count
        ),
    )(owned, target, ids, after)


def split_kernel(in_ref, rows_ref, ids_ref):
    slots, width = rows_ref.shape
    rows_ref[...] = in_ref[:, :, :width].reshape(slots, width)
    tail = in_ref[:, :, width:].reshape(slots, 128).astype(jnp.float32).T
    high, low = tail[0:1, :], tail[64:65, :]
    ids_ref[...] = jnp.where(high == 0.0, -1.0, (high - 1.0) * 128.0 + low).astype(jnp.int32)


def split_rows(arrived):
    devices, cap, wide = arrived.shape
    slots, width = devices * cap, wide - 128
    return pl.pallas_call(
        split_kernel,
        in_specs=vmem(1),
        out_specs=vmem(2),
        out_shape=[
            jax.ShapeDtypeStruct((slots, width), jnp.bfloat16),
            jax.ShapeDtypeStruct((1, slots), jnp.int32),
        ],
        compiler_params=params(),
        name="split",
        cost_estimate=pl.CostEstimate(flops=0, bytes_accessed=4 * slots * width, transcendentals=0),
    )(arrived)


def within_kernel(own0, own1, prior_ref, acc_ref):
    acc_ref[...] = jnp.full(acc_ref.shape, LOWEST, jnp.float32)
    acc_ref[OWN : OWN + 1, :] = prior_ref[...]
    own = [(0, 0), (1, 1)]
    update(acc_ref, OWN, own, own, lambda half: (own0, own1)[half])


def stage(name, own, arrays, heavy_pairs, light_pairs, where, found, after=(), last=False):
    names = list(arrays)
    size, width = arrays[names[0]].shape
    rows = found.shape[1]

    def run(*refs):
        held, refs = dict(zip(("own0", "own1"), refs[: len(own)])), refs[len(own) :]
        inputs, where_ref, so_far_ref = refs[: len(names)], refs[len(names)], refs[len(names) + 1]
        outs, (buffers, sems) = refs[len(names) + 2 + len(after) : -2], refs[-2:]
        acc_ref = outs[-1]
        acc_ref[...] = so_far_ref[...]
        compare(where_ref, 1, acc_ref, held, names, inputs, buffers, sems, heavy_pairs)
        if light_pairs:
            compare(where_ref, 0, acc_ref, held, names, inputs, buffers, sems, light_pairs)
        if last:
            own_out, send_out = outs[:2]
            own_row = acc_ref[OWN : OWN + 1, :]
            from_partner, from_behind = refs[len(names) + 2][...], refs[len(names) + 3][...]
            with_behind = jnp.where(where_ref[0] == 1, jnp.maximum(from_partner, from_behind), from_partner)
            own_out[...] = jnp.where(where_ref[1] == 0, jnp.maximum(own_row, with_behind), own_row)
            near_rows = slice(NEAR, NEAR + 1), slice(NEAR_PARTNER, NEAR_PARTNER + 1)
            sent = jnp.where(where_ref[1] == 1, acc_ref[near_rows[0], :], acc_ref[near_rows[1], :])
            send_out[...] = jnp.where(where_ref[0] == 0, acc_ref[FAR_PARTNER : FAR_PARTNER + 1, :], sent)

    products = sum(len(a[1]) * len(b[1]) for a, b in heavy_pairs) / 4
    return pl.pallas_call(
        run,
        in_specs=vmem(len(own))
        + [pl.BlockSpec(memory_space=pl.ANY)] * len(names)
        + smem()
        + vmem(1)
        + ([pl.BlockSpec(memory_space=pltpu.VMEM if last else pltpu.HBM)] * len(after)),
        out_specs=vmem(3 if last else 1),
        out_shape=[jax.ShapeDtypeStruct((1, rows), jnp.float32)] * (2 if last else 0)
        + [jax.ShapeDtypeStruct(found.shape, jnp.float32)],
        scratch_shapes=[pltpu.VMEM((len(names), size, width), jnp.bfloat16), pltpu.SemaphoreType.DMA((len(names),))],
        compiler_params=params(),
        name=name,
        cost_estimate=pl.CostEstimate(
            flops=int(2 * products * rows * rows * width),
            bytes_accessed=2 * len(names) * size * width,
            transcendentals=0,
        ),
    )(*own, *arrays.values(), where, found, *after)


def body(embeds, doc_ids, prior_max, owned, owned_ids, owner_dest):
    devices = lax.axis_size("grp") * lax.axis_size("blk")
    raw = embeds[0]
    rows, width = raw.shape
    core = lax.axis_index("grp") & 1
    heavy = (lax.axis_index("blk") + core) & 1
    where = jnp.stack([core, heavy]).astype(jnp.int32)

    def step(core):
        return 2 - 4 * core

    def to_heavy(core, heavy, block):
        return None if heavy else block ^ 1

    def to_light(core, heavy, block):
        return block ^ 1 if heavy else None

    def ahead(core, heavy, block):
        return block + step(core)

    def heavy_ahead(core, heavy, block):
        return block + step(core) if heavy else None

    def heavy_back(core, heavy, block):
        return block - step(core) if heavy else None

    own0, own1 = (norm_half(raw, doc_ids, half) for half in range(2))
    partner0 = send(own0, to_heavy)
    near1 = send(own1, ahead)
    partner1 = send(own1, to_heavy)
    near0 = send(own0, heavy_ahead)

    found = pl.pallas_call(
        within_kernel,
        in_specs=vmem(3),
        out_specs=pl.BlockSpec(memory_space=pltpu.VMEM),
        out_shape=jax.ShapeDtypeStruct((8, rows), jnp.float32),
        compiler_params=params(),
        name="within",
        cost_estimate=pl.CostEstimate(
            flops=2 * rows * rows * width, bytes_accessed=2 * rows * width, transcendentals=0
        ),
    )(own0, own1, prior_max)
    outgoing = placed_rows(owned, owner_dest.reshape(1, -1), owned_ids.reshape(1, -1), devices, found)
    next_rows, next_ids = split_rows(lax.all_to_all(outgoing, BOTH, split_axis=0, concat_axis=0, tiled=True))

    far0 = send(partner0, heavy_back)
    near_partner0 = send(partner0, heavy_ahead)
    near_partner1 = send(near1, to_heavy)
    far1 = send(partner1, heavy_back)

    own = (OWN, [(0, "own0"), (1, "own1")])
    partner_both = (PARTNER, [(0, "partner0"), (1, "partner1")])
    near_both = (NEAR, [(0, "near0"), (1, "near1")])
    (found,) = stage(
        "cross_a",
        (own0, own1),
        {"partner0": partner0, "near1": near1, "near0": near0, "partner1": partner1},
        [
            (own, (PARTNER, [(0, "partner0")])),
            (own, near_both),
            ((PARTNER, [(0, "partner0")]), near_both),
            (own, (PARTNER, [(1, "partner1")])),
            ((PARTNER, [(1, "partner1")]), near_both),
        ],
        [(own, (NEAR_PARTNER, [(1, "near1")]))],
        where,
        found,
    )
    (found,) = stage(
        "cross_b",
        (own0, own1),
        {
            "near0": near0,
            "far0": far0,
            "near1": near1,
            "near_partner0": near_partner0,
            "near_partner1": near_partner1,
            "partner0": partner0,
            "partner1": partner1,
        },
        [
            ((FAR_PARTNER, [(0, "far0")]), near_both),
            (own, (NEAR_PARTNER, [(0, "near_partner0"), (1, "near_partner1")])),
            (partner_both, (NEAR_PARTNER, [(0, "near_partner0")])),
        ],
        [],
        where,
        found,
    )
    from_partner = send(found[PARTNER : PARTNER + 1], to_light)
    behind = found[NEAR_PARTNER : NEAR_PARTNER + 1]
    from_behind = send(behind, lambda core, heavy, block: block + 3 if heavy and core else None)
    mine, for_last, _ = stage(
        "cross_c",
        (),
        {"far1": far1, "near0": near0, "near1": near1},
        [((FAR_PARTNER, [(1, "far1")]), near_both)],
        [],
        where,
        found,
        (from_partner, from_behind, next_ids),
        last=True,
    )
    from_last = send(for_last, lambda core, heavy, block: block + 2 if core else (block + 1 if heavy else None))
    gets = (core == 1) | (heavy == 0)
    running = jnp.maximum(mine, jnp.where(gets, from_last, jnp.float32(LOWEST)))
    return (running, next_rows, next_ids.reshape(-1))


def solution(mesh):
    return jax.shard_map(
        body,
        mesh=mesh,
        in_specs=(
            P("grp", "blk", None),
            P("grp", "blk"),
            P("grp", "blk"),
            P(("grp", "blk"), None),
            P(("grp", "blk")),
            P(("grp", "blk"), None),
        ),
        out_specs=(P("grp", "blk"), P(("grp", "blk"), None), P(("grp", "blk"))),
        check_vma=False,
    )
```

```python
import jax
import jax.numpy as jnp
from jax import lax
from jax.experimental import pallas as pl
from jax.experimental.pallas import tpu as pltpu
from jax.sharding import PartitionSpec as P

CAP = 4
LOWEST = -2.0
EXTRA = 16
AHEAD = 3
BOTH = ("grp", "blk")
OWN, PARTNER, NEAR, NEAR_PARTNER, FAR_PARTNER = range(5)


def normalize(matrix):
    values = matrix.astype(jnp.float32)
    scale = lax.rsqrt(jnp.sum(values * values, axis=-1, keepdims=True) + 1e-06)
    return (values * scale).astype(jnp.bfloat16)


def send(value, to):
    groups, members = lax.axis_size("grp"), lax.axis_size("blk")
    pairs = []
    for group in range(groups):
        for block in range(members):
            core = group % 2
            target = to(core, (block + core) % 2 == 1, block)
            if target is not None:
                pairs.append((group * members + block, group * members + target % members))
    return lax.ppermute(value, BOTH, pairs)


def params():
    return pltpu.CompilerParams(vmem_limit_bytes=24 * 1024 * 1024)


def vmem(n):
    return [pl.BlockSpec(memory_space=pltpu.VMEM)] * n


def smem():
    return [pl.BlockSpec(memory_space=pltpu.SMEM)]


def down(row):
    return jnp.broadcast_to(row, (128, row.shape[1])).T


def halves(numbers):
    numbers = numbers.astype(jnp.int32)
    return (numbers >> 7).astype(jnp.float32), (numbers & 127).astype(jnp.float32)


def numbers_of(ref):
    size = ref.shape[0] - EXTRA
    tail = ref[size:, :size].astype(jnp.float32)
    return (tail[0:1, :] * 128.0 + tail[1:2, :]).astype(jnp.int32)


def best(rows, row_ids, cols, col_down):
    scores = lax.dot_general(cols, rows, (((1,), (1,)), ((), ())), preferred_element_type=jnp.float32)
    found = []
    for left in range(0, rows.shape[0], 128):
        keep = col_down < row_ids[:, left : left + 128]
        part = jnp.where(keep, scores[:, left : left + 128], jnp.float32(LOWEST))
        found.append(jnp.max(part, axis=0, keepdims=True))
    return jnp.concatenate(found, axis=1)


def update(acc_ref, at_row, rows, cols, arrive):
    for _, col in cols:
        col_ref = arrive(col)
        size = col_ref.shape[0] - EXTRA
        col_down = down(numbers_of(col_ref))
        for half, row in rows:
            row_ref = arrive(row)
            row_ids = numbers_of(row_ref)
            for top in range(0, size, 256):
                found = best(row_ref[top : top + 256, :], row_ids[:, top : top + 256], col_ref[:size, :], col_down)
                at = slice(half * size + top, half * size + top + 256)
                acc_ref[at_row : at_row + 1, at] = jnp.maximum(acc_ref[at_row : at_row + 1, at], found)


def compare(where_ref, heavy, acc_ref, held, names, refs, buffers, sems, pairs):
    needed = [name for name in names if any(name == n for p in pairs for side in p for _, n in side[1])]

    def run(core):
        copies = {
            name: pltpu.make_async_copy(refs[names.index(name)], buffers.at[k], sems.at[k])
            for k, name in enumerate(needed)
        }
        started, there = set(), set()

        def arrive(name):
            if name in held:
                return held[name]
            if name not in there:
                for k, other in enumerate(needed):
                    if other not in started and k <= needed.index(name) + AHEAD:
                        copies[other].start()
                        started.add(other)
                copies[name].wait()
                there.add(name)
            return buffers.at[needed.index(name)]

        for (first, first_halves), (second, second_halves) in pairs:
            if core == 0:
                update(acc_ref, first, first_halves, second_halves, arrive)
            else:
                update(acc_ref, second, second_halves, first_halves, arrive)

    for core in (0, 1):

        @pl.when((where_ref[0] == core) & (where_ref[1] == heavy))
        def _():
            run(core)


def norm_kernel(x_ref, ids_ref, out_ref):
    size, width = x_ref.shape
    out_ref[:size, :] = normalize(x_ref[...])
    ids = jnp.concatenate([ids_ref[...], jnp.zeros((1, width - size), jnp.int32)], axis=1)
    high, low = halves(ids)
    row = lax.broadcasted_iota(jnp.int32, (EXTRA, width), 0)
    out_ref[size:, :] = jnp.where(row == 0, high, jnp.where(row == 1, low, 0.0)).astype(jnp.bfloat16)


def norm_half(embeds, ids, half):
    rows, width = embeds.shape
    size = rows // 2
    return pl.pallas_call(
        norm_kernel,
        grid=(1,),
        in_specs=[
            pl.BlockSpec((size, width), lambda i: (half, 0)),
            pl.BlockSpec((1, size), lambda i: (0, half)),
        ],
        out_specs=pl.BlockSpec((size + EXTRA, width), lambda i: (0, 0)),
        out_shape=jax.ShapeDtypeStruct((size + EXTRA, width), jnp.bfloat16),
        compiler_params=params(),
        name=f"norm_{half}",
        cost_estimate=pl.CostEstimate(flops=4 * size * width, bytes_accessed=4 * size * width, transcendentals=size),
    )(embeds, ids)


def place_kernel(rows_ref, target_ref, ids_ref, after_ref, out_ref):
    del after_ref
    count, width = rows_ref.shape
    target = target_ref[...]
    across = jnp.broadcast_to(target, (count, count))
    earlier = lax.broadcasted_iota(jnp.int32, (count, count), 0) < lax.broadcasted_iota(
        jnp.int32, (count, count), 1
    )
    same = (across.T == across) & earlier
    position = jnp.sum(same.astype(jnp.float32), axis=0, keepdims=True).astype(jnp.int32)
    place = target * CAP + position
    devices = out_ref.shape[0]
    slots = devices * CAP
    pick = (lax.broadcasted_iota(jnp.int32, (slots, count), 0) == place).astype(jnp.float32).astype(jnp.bfloat16)
    placed = jnp.dot(pick, normalize(rows_ref[...]), preferred_element_type=jnp.float32)
    out_ref[:, :, :width] = placed.astype(jnp.bfloat16).reshape(devices, CAP, width)
    high, low = halves(down(ids_ref[...]))
    lane = lax.broadcasted_iota(jnp.int32, high.shape, 1)
    pair = jnp.where(lane < 64, high + 1.0, low).astype(jnp.bfloat16)
    tail = jnp.dot(pick, pair, preferred_element_type=jnp.float32)
    out_ref[:, :, width:] = tail.astype(jnp.bfloat16).reshape(devices, CAP, 128)


def placed_rows(owned, target, ids, devices, after):
    count, width = owned.shape
    return pl.pallas_call(
        place_kernel,
        in_specs=vmem(4),
        out_specs=pl.BlockSpec(memory_space=pltpu.VMEM),
        out_shape=jax.ShapeDtypeStruct((devices, CAP, width + 128), jnp.bfloat16),
        compiler_params=params(),
        name="place",
        cost_estimate=pl.CostEstimate(
            flops=2 * devices * CAP * count * width, bytes_accessed=2 * (count + devices * CAP) * width, transcendentals=count
        ),
    )(owned, target, ids, after)


def split_kernel(in_ref, rows_ref, ids_ref):
    slots, width = rows_ref.shape
    rows_ref[...] = in_ref[:, :, :width].reshape(slots, width)
    tail = in_ref[:, :, width:].reshape(slots, 128).astype(jnp.float32).T
    high, low = tail[0:1, :], tail[64:65, :]
    ids_ref[...] = jnp.where(high == 0.0, -1.0, (high - 1.0) * 128.0 + low).astype(jnp.int32)


def split_rows(arrived):
    devices, cap, wide = arrived.shape
    slots, width = devices * cap, wide - 128
    return pl.pallas_call(
        split_kernel,
        in_specs=vmem(1),
        out_specs=vmem(2),
        out_shape=[
            jax.ShapeDtypeStruct((slots, width), jnp.bfloat16),
            jax.ShapeDtypeStruct((1, slots), jnp.int32),
        ],
        compiler_params=params(),
        name="split",
        cost_estimate=pl.CostEstimate(flops=0, bytes_accessed=4 * slots * width, transcendentals=0),
    )(arrived)


def within_kernel(own0, own1, prior_ref, acc_ref):
    acc_ref[...] = jnp.full(acc_ref.shape, LOWEST, jnp.float32)
    acc_ref[OWN : OWN + 1, :] = prior_ref[...]
    own = [(0, 0), (1, 1)]
    update(acc_ref, OWN, own, own, lambda half: (own0, own1)[half])


def stage(name, own, arrays, heavy_pairs, light_pairs, where, found, after=(), last=False):
    names = list(arrays)
    size, width = arrays[names[0]].shape
    rows = found.shape[1]

    def run(*refs):
        held, refs = dict(zip(("own0", "own1"), refs[: len(own)])), refs[len(own) :]
        inputs, where_ref, so_far_ref = refs[: len(names)], refs[len(names)], refs[len(names) + 1]
        outs, (buffers, sems) = refs[len(names) + 2 + len(after) : -2], refs[-2:]
        acc_ref = outs[-1]
        acc_ref[...] = so_far_ref[...]
        compare(where_ref, 1, acc_ref, held, names, inputs, buffers, sems, heavy_pairs)
        if light_pairs:
            compare(where_ref, 0, acc_ref, held, names, inputs, buffers, sems, light_pairs)
        if last:
            own_out, send_out = outs[:2]
            own_row = acc_ref[OWN : OWN + 1, :]
            from_partner, from_behind = refs[len(names) + 2][...], refs[len(names) + 3][...]
            with_behind = jnp.where(where_ref[0] == 1, jnp.maximum(from_partner, from_behind), from_partner)
            own_out[...] = jnp.where(where_ref[1] == 0, jnp.maximum(own_row, with_behind), own_row)
            near_rows = slice(NEAR, NEAR + 1), slice(NEAR_PARTNER, NEAR_PARTNER + 1)
            sent = jnp.where(where_ref[1] == 1, acc_ref[near_rows[0], :], acc_ref[near_rows[1], :])
            send_out[...] = jnp.where(where_ref[0] == 0, acc_ref[FAR_PARTNER : FAR_PARTNER + 1, :], sent)

    products = sum(len(a[1]) * len(b[1]) for a, b in heavy_pairs) / 4
    return pl.pallas_call(
        run,
        in_specs=vmem(len(own))
        + [pl.BlockSpec(memory_space=pl.ANY)] * len(names)
        + smem()
        + vmem(1)
        + ([pl.BlockSpec(memory_space=pltpu.VMEM if last else pltpu.HBM)] * len(after)),
        out_specs=vmem(3 if last else 1),
        out_shape=[jax.ShapeDtypeStruct((1, rows), jnp.float32)] * (2 if last else 0)
        + [jax.ShapeDtypeStruct(found.shape, jnp.float32)],
        scratch_shapes=[pltpu.VMEM((len(names), size, width), jnp.bfloat16), pltpu.SemaphoreType.DMA((len(names),))],
        compiler_params=params(),
        name=name,
        cost_estimate=pl.CostEstimate(
            flops=int(2 * products * rows * rows * width),
            bytes_accessed=2 * len(names) * size * width,
            transcendentals=0,
        ),
    )(*own, *arrays.values(), where, found, *after)


def body(embeds, doc_ids, prior_max, owned, owned_ids, owner_dest):
    devices = lax.axis_size("grp") * lax.axis_size("blk")
    raw = embeds[0]
    rows, width = raw.shape
    core = lax.axis_index("grp") & 1
    heavy = (lax.axis_index("blk") + core) & 1
    where = jnp.stack([core, heavy]).astype(jnp.int32)

    def step(core):
        return 2 - 4 * core

    def to_heavy(core, heavy, block):
        return None if heavy else block ^ 1

    def to_light(core, heavy, block):
        return block ^ 1 if heavy else None

    def ahead(core, heavy, block):
        return block + step(core)

    def heavy_ahead(core, heavy, block):
        return block + step(core) if heavy else None

    def heavy_back(core, heavy, block):
        return block - step(core) if heavy else None

    own0, own1 = (norm_half(raw, doc_ids, half) for half in range(2))
    partner0 = send(own0, to_heavy)
    near1 = send(own1, ahead)
    partner1 = send(own1, to_heavy)
    near0 = send(own0, heavy_ahead)

    found = pl.pallas_call(
        within_kernel,
        in_specs=vmem(3),
        out_specs=pl.BlockSpec(memory_space=pltpu.VMEM),
        out_shape=jax.ShapeDtypeStruct((8, rows), jnp.float32),
        compiler_params=params(),
        name="within",
        cost_estimate=pl.CostEstimate(
            flops=2 * rows * rows * width, bytes_accessed=2 * rows * width, transcendentals=0
        ),
    )(own0, own1, prior_max)
    outgoing = placed_rows(owned, owner_dest.reshape(1, -1), owned_ids.reshape(1, -1), devices, found)
    next_rows, next_ids = split_rows(lax.all_to_all(outgoing, BOTH, split_axis=0, concat_axis=0, tiled=True))

    far0 = send(partner0, heavy_back)
    near_partner0 = send(partner0, heavy_ahead)
    near_partner1 = send(near1, to_heavy)
    far1 = send(partner1, heavy_back)

    own = (OWN, [(0, "own0"), (1, "own1")])
    partner_both = (PARTNER, [(0, "partner0"), (1, "partner1")])
    near_both = (NEAR, [(0, "near0"), (1, "near1")])
    (found,) = stage(
        "cross_a",
        (own0, own1),
        {"partner0": partner0, "near1": near1, "near0": near0, "partner1": partner1},
        [
            (own, (PARTNER, [(0, "partner0")])),
            (own, near_both),
            ((PARTNER, [(0, "partner0")]), near_both),
            (own, (PARTNER, [(1, "partner1")])),
            ((PARTNER, [(1, "partner1")]), near_both),
        ],
        [(own, (NEAR_PARTNER, [(1, "near1")]))],
        where,
        found,
    )
    (found,) = stage(
        "cross_b",
        (own0, own1),
        {
            "near0": near0,
            "far0": far0,
            "near1": near1,
            "near_partner0": near_partner0,
            "near_partner1": near_partner1,
            "partner0": partner0,
            "partner1": partner1,
        },
        [
            ((FAR_PARTNER, [(0, "far0")]), near_both),
            (own, (NEAR_PARTNER, [(0, "near_partner0"), (1, "near_partner1")])),
            (partner_both, (NEAR_PARTNER, [(0, "near_partner0")])),
        ],
        [],
        where,
        found,
        (next_ids,),
    )
    from_partner = send(found[PARTNER : PARTNER + 1], to_light)
    behind = found[NEAR_PARTNER : NEAR_PARTNER + 1]
    from_behind = send(behind, lambda core, heavy, block: block + 3 if heavy and core else None)
    mine, for_last, _ = stage(
        "cross_c",
        (),
        {"far1": far1, "near0": near0, "near1": near1},
        [((FAR_PARTNER, [(1, "far1")]), near_both)],
        [],
        where,
        found,
        (from_partner, from_behind),
        last=True,
    )
    from_last = send(for_last, lambda core, heavy, block: block + 2 if core else (block + 1 if heavy else None))
    gets = (core == 1) | (heavy == 0)
    running = jnp.maximum(mine, jnp.where(gets, from_last, jnp.float32(LOWEST)))
    return (running, next_rows, next_ids.reshape(-1))


def solution(mesh):
    return jax.shard_map(
        body,
        mesh=mesh,
        in_specs=(
            P("grp", "blk", None),
            P("grp", "blk"),
            P("grp", "blk"),
            P(("grp", "blk"), None),
            P(("grp", "blk")),
            P(("grp", "blk"), None),
        ),
        out_specs=(P("grp", "blk"), P(("grp", "blk"), None), P(("grp", "blk"))),
        check_vma=False,
    )
```
